256 devices in a mesh: ctx: 64 (over y_hi, z, x), head: 4 (over y_lo, core).
Axes of the slice: x: 4, y: 4 (y_hi: 2, y_lo: 2; y = y_hi * 2 + y_lo), z: 8, core: 2. Of those that a mesh axis runs over, the one named last changes fastest.
Arguments:
- query_rows: bfloat16 [16384, 8192], P('ctx', 'head'), may hold values from -64 to 64, as said below
- key_rows: bfloat16 [16384, 512], P('ctx', 'head'), may hold values from -5 to 5
- value_rows: bfloat16 [16384, 512], P('ctx', 'head'), may hold values from -6 to 6
- kept_rows: int32 [64, 4, 64], P('ctx', 'head'), may hold values from 0 to 255
Outputs:
- attended: bfloat16 [16384, 8192], P(('ctx', 'head'))
The draws below stay inside these ranges and needn't reach their ends.
Inputs may be any that keep to these rules, and one draw needn't show every extreme that they name: `query_rows`: queries in the range of the table; heads of one position may be large multiples of that position's key.
All inputs are finite; a program needn't handle non-finite values.
Results may differ from the reference program's by a relative error of at most 0.012.
Values may be sent and summed in bfloat16 or wider, within the bound.
A program may use at most 128 MiB of HBM per device.

```python
import math
import jax
import jax.numpy as jnp
from jax import lax

HD = 128
KVH = 4
GROUP = 16
BLK = 256
KEEP = 64
ANCHOR = 256
SHARDS = 64
TOKENS = 16384
QH = 64


def draw_key_rows(key, part):
    key = jax.random.fold_in(key, 5)
    result = jnp.clip(jax.random.normal(key, (TOKENS, KVH * HD), jnp.float32), -5.0, 5.0)
    return result.astype(jnp.bfloat16)


def draw_query_rows(key, part):
    key = jax.random.fold_in(key, 3)
    result = jnp.clip(2.5 * jax.random.normal(key, (TOKENS, QH * HD), jnp.float32), -12.0, 12.0)
    return result.astype(jnp.bfloat16)


def touch_ends(values, own_key, low, high):
    dims = values.shape
    spot = [jax.random.randint(jax.random.fold_in(own_key, axis), (), 0, dims[axis]) for axis in range(len(dims))]
    values = values.at[tuple(spot)].set(low)
    longest = dims.index(max(dims))
    spot[longest] = (spot[longest] + 1) % dims[longest]
    return values.at[tuple(spot)].set(high)


def steps_of(own_key, extent, pieces, smallest, high):
    level, own = 1.0, jax.random.fold_in(own_key, 6)
    for axis_at, shards_of in pieces:
        steps = jnp.exp(jax.random.uniform(jax.random.fold_in(own, axis_at), (shards_of,), jnp.float32, smallest / len(pieces), high / len(pieces)))
        level = level * jnp.repeat(steps, extent[axis_at] // shards_of).reshape([-1 if axis == axis_at else 1 for axis in range(len(extent))])
    return level


def scatter_about(key, shape, scale, limit, pieces=(), kind=jnp.bfloat16):
    array = jax.random.normal(key, shape, jnp.float32) * scale
    if len(pieces) > 0:
        array = steps_of(key, shape, pieces, -0.22, 0.18) * array
    return jnp.clip(array, min=-limit, max=limit).astype(kind)


def setup_inputs(seed: int = 0) -> dict:
    arg_keys = jax.random.split(jax.random.key(seed), 5)
    return {
        "query_rows": draw_query_rows(jax.random.fold_in(arg_keys[4], 71), 0),
        "key_rows": draw_key_rows(jax.random.fold_in(arg_keys[4], 71), 0),
        "value_rows": scatter_about(arg_keys[2], (TOKENS, KVH * HD), 1.0, 6.0, ((0, 64), (1, 4))),
        "kept_rows": touch_ends(jax.random.randint(arg_keys[3], (SHARDS, KVH, KEEP), 0, BLK), jax.random.fold_in(arg_keys[3], 1), 0, BLK - 1).astype(jnp.int32),
    }


def reference(query_rows, key_rows, value_rows, kept_rows):
    factor = 1.0 / math.sqrt(HD)
    key_blocks = key_rows.reshape(SHARDS, BLK, KVH, HD).transpose(0, 2, 1, 3)
    value_blocks = value_rows.reshape(SHARDS, BLK, KVH, HD).transpose(0, 2, 1, 3)
    query_blocks = query_rows.reshape(SHARDS, BLK, KVH, GROUP, HD).transpose(0, 2, 1, 3, 4)
    picked = kept_rows.astype(jnp.int32)[:, :, :, None]
    compact_keys = jnp.take_along_axis(key_blocks, picked, axis=2)
    compact_values = jnp.take_along_axis(value_blocks, picked, axis=2)
    anchor_keys = key_blocks[0, :, :ANCHOR]
    anchor_values = value_blocks[0, :, :ANCHOR]
    causal = jnp.arange(BLK, dtype=jnp.int32)[None, :] <= jnp.arange(BLK, dtype=jnp.int32)[:, None]
    shard_ids = jnp.arange(SHARDS * KEEP, dtype=jnp.int32) // KEEP

    def single(item):
        shard = item // KVH
        head_group = item % KVH
        queries = query_blocks[shard, head_group].astype(jnp.float32)
        keys_all = jnp.concatenate([key_blocks[shard, head_group], anchor_keys[head_group], compact_keys[:, head_group].reshape(SHARDS * KEEP, HD)], axis=0).astype(jnp.float32)
        values_all = jnp.concatenate([value_blocks[shard, head_group], anchor_values[head_group], compact_values[:, head_group].reshape(SHARDS * KEEP, HD)], axis=0).astype(jnp.float32)
        allowed = jnp.concatenate([causal, jnp.broadcast_to(shard > 0, (BLK, ANCHOR)), jnp.broadcast_to((shard_ids < shard)[None, :], (BLK, SHARDS * KEEP))], axis=1)
        scores = jnp.einsum('thd,sd->ths', queries, keys_all) * factor
        scores = jnp.where(allowed[:, None, :], scores, -jnp.inf)
        largest = scores.max(axis=2, keepdims=True)
        weights = jnp.exp(scores - largest)
        totals = weights.sum(axis=2)
        rounded = lax.optimization_barrier(weights.astype(jnp.bfloat16)).astype(jnp.float32)
        mixed = jnp.einsum('ths,sd->thd', rounded, values_all)
        return (mixed / totals[..., None]).astype(jnp.bfloat16)
    outputs = lax.map(single, jnp.arange(SHARDS * KVH, dtype=jnp.int32))
    outputs = outputs.reshape(SHARDS, KVH, BLK, GROUP, HD).transpose(0, 2, 1, 3, 4)
    return outputs.reshape(SHARDS * BLK, KVH * GROUP * HD)
```

```python
import functools
import math

import jax
import jax.numpy as jnp
from jax import lax
from jax.experimental import pallas as pl
from jax.experimental.pallas import tpu as pltpu
from jax.sharding import PartitionSpec as P

MESH = pl.DeviceIdType.MESH
HD = 128
BLK = 256
KEEP = 64
GROUP = 16
PAIR = 2
ITEMS = GROUP // PAIR
COLS = PAIR * BLK
FULL = 16
FULL_KEYS = FULL * KEEP
LAST_KEYS = FULL_KEYS + BLK
VROWS = 144
AROWS = 136
SCALE = math.log2(math.e) / math.sqrt(HD)
LOW = -1e30


def dot_t(a, b):
    return lax.dot_general(a, b, (((1,), (1,)), ((), ())), preferred_element_type=jnp.float32)


def kernel(
    shards, heads, q_ref, k_ref, v_ref, kept_ref, out_ref,
    compact, slots, anchor, kc, vt, s0, s1, p0, p1, mx, al, m_ref, acc_ref, obuf,
    send_sem, recv_sem, anchor_send, anchor_recv, out_send, out_recv, own_sem,
):
    me = lax.axis_index("ctx")
    head = lax.axis_index("head")
    scores, probs = (s0, s1), (p0, p1)

    barrier = pltpu.get_barrier_semaphore()

    def greet(c, carry):
        pl.semaphore_signal(barrier, inc=1, device_id=(c, head), device_id_type=MESH)
        return carry

    lax.fori_loop(0, me, greet, 0)
    for step in range(1, heads):
        peer = lax.rem(head + step, heads)
        pl.semaphore_signal(barrier, inc=1, device_id=(me, peer), device_id_type=MESH)

    chosen = (
        lax.broadcasted_iota(jnp.int32, (BLK, KEEP), 0) == kept_ref[...]
    ).astype(jnp.bfloat16)
    for part, ref in ((0, k_ref), (HD, v_ref)):
        picked = lax.dot_general(
            chosen, ref[...], (((0,), (0,)), ((), ())), preferred_element_type=jnp.float32
        )
        compact[:, part : part + HD] = picked.astype(jnp.bfloat16)

    @pl.when(me == 0)
    def _():
        anchor[:, :HD] = k_ref[...]
        anchor[:, HD:] = v_ref[...]

    slots[0:FULL] = jnp.concatenate(
        [
            jnp.broadcast_to(k_ref[0:1, :], (FULL * KEEP, HD)),
            jnp.zeros((FULL * KEEP, HD), jnp.bfloat16),
        ],
        axis=1,
    ).reshape(FULL, KEEP, 2 * HD)

    pl.semaphore_wait(barrier, shards - 1 - me + heads - 1)

    def block_copy(target):
        return pltpu.make_async_remote_copy(
            src_ref=compact,
            dst_ref=slots.at[FULL + me],
            send_sem=send_sem.at[target],
            recv_sem=recv_sem.at[me],
            device_id=(target, head),
            device_id_type=MESH,
        )

    def send_block(target, carry):
        block_copy(target).start()
        return carry

    lax.fori_loop(me + 1, shards, send_block, 0)

    def anchor_copy(stage, step, stride):
        return pltpu.make_async_remote_copy(
            src_ref=anchor,
            dst_ref=anchor,
            send_sem=anchor_send.at[stage, step - 1],
            recv_sem=anchor_recv,
            device_id=(me + step * stride, head),
            device_id_type=MESH,
        )

    def relay(stage, stride):
        for step in range(1, 4):
            anchor_copy(stage, step, stride).start()

    def wait_anchor():
        pltpu.make_async_copy(anchor, anchor, anchor_recv).wait()

    @pl.when(me == 0)
    def _():
        relay(0, 16)

    def score(item, slot, keys, own):
        q = q_ref[:, pl.ds(pl.multiple_of(item * PAIR * HD, HD), PAIR * HD)]
        q = jnp.concatenate([q[:, j * HD : (j + 1) * HD] for j in range(PAIR)], axis=0)
        s = dot_t(kc[0:keys], q) * SCALE
        if own:
            row = lax.broadcasted_iota(jnp.int32, (BLK, COLS), 0)
            col = lax.broadcasted_iota(jnp.int32, (BLK, COLS), 1)
            s = jnp.where(row <= jnp.bitwise_and(col, BLK - 1), s, LOW)
        scores[slot][0:keys] = s
        mx[slot] = jnp.broadcast_to(s.max(axis=0, keepdims=True), (8, COLS))

    def weigh(item, slot, keys, own):
        peak = mx[slot]
        if not own:
            before = m_ref[item]
            peak = jnp.maximum(before, peak)
            al[slot] = jnp.exp2(before - peak)
        m_ref[item] = peak
        probs[slot][0:keys] = jnp.exp2(scores[slot][0:keys] - peak[0:1]).astype(jnp.bfloat16)

    def mix(item, slot, keys, own):
        pv = jnp.dot(vt[:, 0:keys], probs[slot][0:keys], preferred_element_type=jnp.float32)
        pv = pv[:AROWS]
        if not own:
            pv = acc_ref[item] * al[slot, 0:1] + pv
        acc_ref[item] = pv

    def out_copy(item, step):
        peer = lax.rem(head + step, heads)
        rows = BLK // heads
        columns = pl.ds(pl.multiple_of((head * GROUP + item * PAIR) * HD, HD), PAIR * HD)
        return pltpu.make_async_remote_copy(
            src_ref=obuf.at[item, pl.ds(pl.multiple_of(peer * rows, rows), rows)],
            dst_ref=out_ref.at[:, columns],
            send_sem=out_send.at[item, step - 1],
            recv_sem=out_recv.at[item, step - 1],
            device_id=(me, peer),
            device_id_type=MESH,
        )

    def own_copy(item):
        rows = BLK // heads
        columns = pl.ds(pl.multiple_of((head * GROUP + item * PAIR) * HD, HD), PAIR * HD)
        return pltpu.make_async_copy(
            obuf.at[item, pl.ds(pl.multiple_of(head * rows, rows), rows)],
            out_ref.at[:, columns],
            own_sem.at[item],
        )

    def emit(item):
        a = acc_ref[item]
        o = (a[:HD] / a[HD : HD + 1]).T.astype(jnp.bfloat16)
        for j in range(PAIR):
            obuf[item, :, j * HD : (j + 1) * HD] = o[j * BLK : (j + 1) * BLK]
        for step in range(1, heads):
            out_copy(item, step).start()
        own_copy(item).start()

    def phase(keys, own=False, last=False):
        def mixed(item, slot):
            mix(item, slot, keys, own)
            if last:
                emit(item)

        score(0, 0, keys, own)
        weigh(0, 0, keys, own)
        score(1, 1, keys, own)

        def body(g, carry):
            t = 2 * g
            for b in range(2):
                mix(t + b, b, keys, own)
                weigh(t + b + 1, 1 - b, keys, own)
                score(t + b + 2, b, keys, own)
                if last:
                    emit(t + b)
            return carry

        lax.fori_loop(0, ITEMS // 2 - 1, body, 0)
        mixed(ITEMS - 2, 0)
        weigh(ITEMS - 1, 1, keys, own)
        mixed(ITEMS - 1, 1)

    kc[0:BLK] = k_ref[...]
    vt[0:HD, 0:BLK] = v_ref[...].T
    vt[HD:VROWS, 0:BLK] = jnp.ones((VROWS - HD, BLK), jnp.bfloat16)
    phase(BLK, own=True)

    @pl.when(lax.rem(me, 16) == 0)
    def _():
        @pl.when(me > 0)
        def _():
            wait_anchor()

        relay(1, 4)

    def wait_slot(slot, carry):
        pltpu.make_async_copy(compact, slots.at[FULL + slot], recv_sem.at[slot]).wait()
        return carry

    def load_chunk(first):
        lax.fori_loop(jnp.maximum(first, 0), first + FULL, wait_slot, 0)
        part = slots[pl.ds(first + FULL, FULL)]
        part = part.reshape(FULL_KEYS, 2 * HD)
        kc[0:FULL_KEYS] = part[:, :HD]
        valid = lax.broadcasted_iota(jnp.int32, (VROWS - HD, FULL_KEYS), 1) >= -first * KEEP
        vt[0:HD, 0:FULL_KEYS] = part[:, HD:].T
        vt[HD:VROWS, 0:FULL_KEYS] = valid.astype(jnp.bfloat16)

    full_chunks = lax.div(jnp.maximum(me - 1, 0), FULL)

    def full_chunk(j, carry):
        load_chunk(me - FULL * (j + 1))
        phase(FULL_KEYS)
        return carry

    lax.fori_loop(0, jnp.minimum(full_chunks, 1), full_chunk, 0)

    @pl.when(lax.rem(me, 4) == 0)
    def _():
        @pl.when(lax.rem(me, 16) > 0)
        def _():
            wait_anchor()

        relay(2, 1)

    lax.fori_loop(1, full_chunks, full_chunk, 0)

    @pl.when(me > 0)
    def _():
        load_chunk(me - FULL * (full_chunks + 1))

        @pl.when(lax.rem(me, 4) > 0)
        def _():
            wait_anchor()

        kc[FULL_KEYS:LAST_KEYS] = anchor[:, :HD]
        vt[0:HD, FULL_KEYS:LAST_KEYS] = anchor[:, HD:].T
        vt[HD:VROWS, FULL_KEYS:LAST_KEYS] = jnp.ones((VROWS - HD, BLK), jnp.bfloat16)
        phase(LAST_KEYS, last=True)

    @pl.when(me == 0)
    def _():
        for item in range(ITEMS):
            emit(item)

    def sent_block(target, carry):
        block_copy(target).wait_send()
        return carry

    lax.fori_loop(me + 1, shards, sent_block, 0)
    for stage, stride in ((0, 16), (1, 4), (2, 1)):
        relays = me == 0 if stage == 0 else lax.rem(me, 4 * stride) == 0

        @pl.when(relays)
        def _():
            for step in range(1, 4):
                anchor_copy(stage, step, stride).wait_send()

    for item in range(ITEMS):
        own_copy(item).wait()
        for step in range(1, heads):
            out_copy(item, step).wait()


def per_device(shards, heads, query_rows, key_rows, value_rows, kept_rows):
    vmem = pl.BlockSpec(memory_space=pltpu.VMEM)
    rows = BLK // heads
    f32, bf16, dma = jnp.float32, jnp.bfloat16, pltpu.SemaphoreType.DMA
    return pl.pallas_call(
        functools.partial(kernel, shards, heads),
        out_shape=jax.ShapeDtypeStruct((rows, heads * GROUP * HD), bf16),
        in_specs=[vmem] * 4,
        out_specs=pl.BlockSpec(memory_space=pl.ANY),
        scratch_shapes=[
            pltpu.VMEM((KEEP, 2 * HD), bf16),
            pltpu.VMEM((FULL + shards, KEEP, 2 * HD), bf16),
            pltpu.VMEM((BLK, 2 * HD), bf16),
            pltpu.VMEM((LAST_KEYS, HD), bf16),
            pltpu.VMEM((VROWS, LAST_KEYS), bf16),
            pltpu.VMEM((LAST_KEYS, COLS), f32),
            pltpu.VMEM((LAST_KEYS, COLS), f32),
            pltpu.VMEM((LAST_KEYS, COLS), bf16),
            pltpu.VMEM((LAST_KEYS, COLS), bf16),
            pltpu.VMEM((2, 8, COLS), f32),
            pltpu.VMEM((2, 8, COLS), f32),
            pltpu.VMEM((ITEMS, 8, COLS), f32),
            pltpu.VMEM((ITEMS, AROWS, COLS), f32),
            pltpu.VMEM((ITEMS, BLK, PAIR * HD), bf16),
            dma((shards,)),
            dma((shards,)),
            dma((3, 3)),
            dma,
            dma((ITEMS, heads - 1)),
            dma((ITEMS, heads - 1)),
            dma((ITEMS,)),
        ],
        compiler_params=pltpu.CompilerParams(
            collective_id=0, has_side_effects=True, vmem_limit_bytes=48 * 2**20
        ),
    )(query_rows, key_rows, value_rows, kept_rows.reshape(1, KEEP))


def solution(mesh):
    shards, heads = mesh.shape["ctx"], mesh.shape["head"]
    return jax.shard_map(
        functools.partial(per_device, shards, heads),
        mesh=mesh,
        in_specs=(P("ctx", "head"), P("ctx", "head"), P("ctx", "head"), P("ctx", "head", None)),
        out_specs=P(("ctx", "head"), None),
        check_vma=False,
    )
```

```python
import functools
import math

import jax
import jax.numpy as jnp
from jax import lax
from jax.experimental import pallas as pl
from jax.experimental.pallas import tpu as pltpu
from jax.sharding import PartitionSpec as P

MESH = pl.DeviceIdType.MESH
HD = 128
BLK = 256
KEEP = 64
GROUP = 16
PAIR = 2
ITEMS = GROUP // PAIR
COLS = PAIR * BLK
WIDTH = 4
FULL = 16
FULL_KEYS = FULL * KEEP
LAST_KEYS = FULL_KEYS + BLK
VROWS = 144
AROWS = 136
SCALE = math.log2(math.e) / math.sqrt(HD)
LOW = -1e30


def dot_t(a, b):
    return lax.dot_general(a, b, (((1,), (1,)), ((), ())), preferred_element_type=jnp.float32)


def kernel(
    shards, heads, q_hbm, k_hbm, v_hbm, kept_hbm, out_ref,
    q_ref, k_ref, v_ref, kept_ref,
    compact, slots, anchor, kc, vt, s0, s1, p0, p1, mx, al, m_ref, acc_ref, obuf,
    load_sem, send_sem, recv_sem, relay_send, anchor_send, anchor_recv, out_send, out_recv, own_sem,
):
    me = lax.axis_index("ctx")
    head = lax.axis_index("head")
    rows = shards // WIDTH
    row, col = lax.div(me, WIDTH), lax.rem(me, WIDTH)
    scores, probs = (s0, s1), (p0, p1)

    barrier = pltpu.get_barrier_semaphore()

    def greet(block, to_head):
        pl.semaphore_signal(barrier, inc=1, device_id=(block, to_head), device_id_type=MESH)

    def mate(step):
        return row * WIDTH + lax.rem(col + step, WIDTH)

    def greet_row(r, carry):
        greet(r * WIDTH + col, head)
        return carry

    lax.fori_loop(0, row, greet_row, 0)
    for step in range(1, WIDTH):
        greet(mate(step), head)
    for step in range(1, heads):
        greet(me, lax.rem(head + step, heads))

    loads = [
        pltpu.make_async_copy(src, dst, load_sem.at[n])
        for n, (src, dst) in enumerate(
            ((kept_hbm, kept_ref), (k_hbm, k_ref), (v_hbm, v_ref), (q_hbm, q_ref))
        )
    ]
    for load in loads:
        load.start()
    for load in loads[:3]:
        load.wait()

    chosen = (
        lax.broadcasted_iota(jnp.int32, (BLK, KEEP), 0) == kept_ref[...]
    ).astype(jnp.bfloat16)
    for part, ref in ((0, k_ref), (HD, v_ref)):
        picked = lax.dot_general(
            chosen, ref[...], (((0,), (0,)), ((), ())), preferred_element_type=jnp.float32
        )
        compact[:, part : part + HD] = picked.astype(jnp.bfloat16)

    @pl.when(me == 0)
    def _():
        anchor[:, :HD] = k_ref[...]
        anchor[:, HD:] = v_ref[...]

    pl.semaphore_wait(barrier, rows - 1 - row + WIDTH - 1 + heads - 1)

    def block_copy(target):
        return pltpu.make_async_remote_copy(
            src_ref=compact,
            dst_ref=slots.at[col, row],
            send_sem=send_sem.at[target],
            recv_sem=recv_sem.at[col, row],
            device_id=(target, head),
            device_id_type=MESH,
        )

    def send_mate(target, carry):
        block_copy(target).start()
        return carry

    def send_row(r, carry):
        block_copy(r * WIDTH + col).start()
        return carry

    lax.fori_loop(me + 1, (row + 1) * WIDTH, send_mate, 0)
    lax.fori_loop(row + 1, rows, send_row, 0)

    filler = jnp.concatenate(
        [jnp.broadcast_to(k_ref[0:1, :], (KEEP, HD)), jnp.zeros((KEEP, HD), jnp.bfloat16)], axis=1
    )

    def fill_mate(c, carry):
        slots[c, row] = filler
        return carry

    def fill_row(r, carry):
        for c in range(WIDTH):
            slots[c, r] = filler
        return carry

    lax.fori_loop(col, WIDTH, fill_mate, 0)
    lax.fori_loop(row + 1, rows, fill_row, 0)

    def anchor_copy(stage, step, stride):
        return pltpu.make_async_remote_copy(
            src_ref=anchor,
            dst_ref=anchor,
            send_sem=anchor_send.at[stage, step - 1],
            recv_sem=anchor_recv,
            device_id=(me + step * stride, head),
            device_id_type=MESH,
        )

    def relay_anchor(stage, stride):
        for step in range(1, 4):
            anchor_copy(stage, step, stride).start()

    def wait_anchor():
        pltpu.make_async_copy(anchor, anchor, anchor_recv).wait()

    @pl.when(me == 0)
    def _():
        relay_anchor(0, 16)

    loads[3].wait()

    def score(item, slot, keys, own):
        q = q_ref[:, pl.ds(pl.multiple_of(item * PAIR * HD, HD), PAIR * HD)]
        q = jnp.concatenate([q[:, j * HD : (j + 1) * HD] for j in range(PAIR)], axis=0)
        s = dot_t(kc[0:keys], q) * SCALE
        if own:
            row = lax.broadcasted_iota(jnp.int32, (BLK, COLS), 0)
            col = lax.broadcasted_iota(jnp.int32, (BLK, COLS), 1)
            s = jnp.where(row <= jnp.bitwise_and(col, BLK - 1), s, LOW)
        scores[slot][0:keys] = s
        mx[slot] = jnp.broadcast_to(s.max(axis=0, keepdims=True), (8, COLS))

    def weigh(item, slot, keys, own):
        peak = mx[slot]
        if not own:
            before = m_ref[item]
            peak = jnp.maximum(before, peak)
            al[slot] = jnp.exp2(before - peak)
        m_ref[item] = peak
        probs[slot][0:keys] = jnp.exp2(scores[slot][0:keys] - peak[0:1]).astype(jnp.bfloat16)

    def mix(item, slot, keys, own):
        pv = jnp.dot(vt[:, 0:keys], probs[slot][0:keys], preferred_element_type=jnp.float32)
        pv = pv[:AROWS]
        if not own:
            pv = acc_ref[item] * al[slot, 0:1] + pv
        acc_ref[item] = pv

    def out_copy(item, step):
        peer = lax.rem(head + step, heads)
        share = BLK // heads
        columns = pl.ds(pl.multiple_of((head * GROUP + item * PAIR) * HD, HD), PAIR * HD)
        return pltpu.make_async_remote_copy(
            src_ref=obuf.at[item, pl.ds(pl.multiple_of(peer * share, share), share)],
            dst_ref=out_ref.at[:, columns],
            send_sem=out_send.at[item, step - 1],
            recv_sem=out_recv.at[item, step - 1],
            device_id=(me, peer),
            device_id_type=MESH,
        )

    def own_copy(item):
        share = BLK // heads
        columns = pl.ds(pl.multiple_of((head * GROUP + item * PAIR) * HD, HD), PAIR * HD)
        return pltpu.make_async_copy(
            obuf.at[item, pl.ds(pl.multiple_of(head * share, share), share)],
            out_ref.at[:, columns],
            own_sem.at[item],
        )

    def emit(item):
        a = acc_ref[item]
        o = (a[:HD] / a[HD : HD + 1]).T.astype(jnp.bfloat16)
        for j in range(PAIR):
            obuf[item, :, j * HD : (j + 1) * HD] = o[j * BLK : (j + 1) * BLK]
        for step in range(1, heads):
            out_copy(item, step).start()
        own_copy(item).start()

    def phase(keys, own=False, last=False):
        def mixed(item, slot):
            mix(item, slot, keys, own)
            if last:
                emit(item)

        score(0, 0, keys, own)
        weigh(0, 0, keys, own)
        score(1, 1, keys, own)

        def body(g, carry):
            t = 2 * g
            for b in range(2):
                mix(t + b, b, keys, own)
                weigh(t + b + 1, 1 - b, keys, own)
                score(t + b + 2, b, keys, own)
                if last:
                    emit(t + b)
            return carry

        lax.fori_loop(0, ITEMS // 2 - 1, body, 0)
        mixed(ITEMS - 2, 0)
        weigh(ITEMS - 1, 1, keys, own)
        mixed(ITEMS - 1, 1)

    kc[0:BLK] = k_ref[...]
    vt[0:HD, 0:BLK] = v_ref[...].T
    vt[HD:VROWS, 0:BLK] = jnp.ones((VROWS - HD, BLK), jnp.bfloat16)
    phase(BLK, own=True)

    @pl.when(lax.rem(me, 16) == 0)
    def _():
        @pl.when(me > 0)
        def _():
            wait_anchor()

        relay_anchor(1, 4)

    def wait_slot(c, r):
        pltpu.make_async_copy(compact, slots.at[c, r], recv_sem.at[c, r]).wait()

    def relay_copy(r, step):
        return pltpu.make_async_remote_copy(
            src_ref=slots.at[col, r],
            dst_ref=slots.at[col, r],
            send_sem=relay_send.at[r, step - 1],
            recv_sem=recv_sem.at[col, r],
            device_id=(mate(step), head),
            device_id_type=MESH,
        )

    def relay(n, carry):
        r = row - 1 - n
        wait_slot(col, r)
        for step in (1, 3, 2):
            relay_copy(r, step).start()
        return carry

    lax.fori_loop(0, row, relay, 0)

    def load_chunk(c):
        part = slots[c].reshape(FULL_KEYS, 2 * HD)
        kc[0:FULL_KEYS] = part[:, :HD]
        count = row + (c < col).astype(jnp.int32)
        valid = lax.broadcasted_iota(jnp.int32, (VROWS - HD, FULL_KEYS), 1) < count * KEEP
        vt[0:HD, 0:FULL_KEYS] = part[:, HD:].T
        vt[HD:VROWS, 0:FULL_KEYS] = valid.astype(jnp.bfloat16)

    def wait_rows(c):
        def body(r, carry):
            wait_slot(c, r)
            return carry

        lax.fori_loop(0, row, body, 0)

        @pl.when(c < col)
        def _():
            wait_slot(c, row)

    @pl.when(me > 0)
    def _():
        load_chunk(col)
        phase(FULL_KEYS)

    @pl.when(lax.rem(me, 4) == 0)
    def _():
        @pl.when(lax.rem(me, 16) > 0)
        def _():
            wait_anchor()

        relay_anchor(2, 1)

    @pl.when(me > 0)
    def _():
        def chunk(step, carry):
            c = lax.rem(col + 2 * step - 1, WIDTH)
            wait_rows(c)
            load_chunk(c)
            phase(FULL_KEYS)
            return carry

        lax.fori_loop(1, 3, chunk, 0)
        c = lax.rem(col + 2, WIDTH)
        wait_rows(c)
        load_chunk(c)

        @pl.when(lax.rem(me, 4) > 0)
        def _():
            wait_anchor()

        kc[FULL_KEYS:LAST_KEYS] = anchor[:, :HD]
        vt[0:HD, FULL_KEYS:LAST_KEYS] = anchor[:, HD:].T
        vt[HD:VROWS, FULL_KEYS:LAST_KEYS] = jnp.ones((VROWS - HD, BLK), jnp.bfloat16)
        phase(LAST_KEYS, last=True)

    @pl.when(me == 0)
    def _():
        for item in range(ITEMS):
            emit(item)

    def sent_mate(target, carry):
        block_copy(target).wait_send()
        return carry

    def sent_row(r, carry):
        block_copy(r * WIDTH + col).wait_send()
        return carry

    def relayed(r, carry):
        for step in range(1, WIDTH):
            relay_copy(r, step).wait_send()
        return carry

    lax.fori_loop(me + 1, (row + 1) * WIDTH, sent_mate, 0)
    lax.fori_loop(row + 1, rows, sent_row, 0)
    lax.fori_loop(0, row, relayed, 0)
    for stage, stride in ((0, 16), (1, 4), (2, 1)):
        relays = me == 0 if stage == 0 else lax.rem(me, 4 * stride) == 0

        @pl.when(relays)
        def _():
            for step in range(1, 4):
                anchor_copy(stage, step, stride).wait_send()

    for item in range(ITEMS):
        own_copy(item).wait()
        for step in range(1, heads):
            out_copy(item, step).wait()


def per_device(shards, heads, query_rows, key_rows, value_rows, kept_rows):
    rows, depth = BLK // heads, shards // WIDTH
    f32, bf16, dma = jnp.float32, jnp.bfloat16, pltpu.SemaphoreType.DMA
    return pl.pallas_call(
        functools.partial(kernel, shards, heads),
        out_shape=jax.ShapeDtypeStruct((rows, heads * GROUP * HD), bf16),
        in_specs=[pl.BlockSpec(memory_space=pl.ANY)] * 4,
        out_specs=pl.BlockSpec(memory_space=pl.ANY),
        scratch_shapes=[
            pltpu.VMEM((BLK, GROUP * HD), bf16),
            pltpu.VMEM((BLK, HD), bf16),
            pltpu.VMEM((BLK, HD), bf16),
            pltpu.VMEM((1, KEEP), jnp.int32),
            pltpu.VMEM((KEEP, 2 * HD), bf16),
            pltpu.VMEM((WIDTH, depth, KEEP, 2 * HD), bf16),
            pltpu.VMEM((BLK, 2 * HD), bf16),
            pltpu.VMEM((LAST_KEYS, HD), bf16),
            pltpu.VMEM((VROWS, LAST_KEYS), bf16),
            pltpu.VMEM((LAST_KEYS, COLS), f32),
            pltpu.VMEM((LAST_KEYS, COLS), f32),
            pltpu.VMEM((LAST_KEYS, COLS), bf16),
            pltpu.VMEM((LAST_KEYS, COLS), bf16),
            pltpu.VMEM((2, 8, COLS), f32),
            pltpu.VMEM((2, 8, COLS), f32),
            pltpu.VMEM((ITEMS, 8, COLS), f32),
            pltpu.VMEM((ITEMS, AROWS, COLS), f32),
            pltpu.VMEM((ITEMS, BLK, PAIR * HD), bf16),
            dma((4,)),
            dma((shards,)),
            dma((WIDTH, depth)),
            dma((depth, WIDTH - 1)),
            dma((3, 3)),
            dma,
            dma((ITEMS, heads - 1)),
            dma((ITEMS, heads - 1)),
            dma((ITEMS,)),
        ],
        compiler_params=pltpu.CompilerParams(
            collective_id=0, has_side_effects=True, vmem_limit_bytes=48 * 2**20
        ),
    )(query_rows, key_rows, value_rows, kept_rows.reshape(1, KEEP))


def solution(mesh):
    shards, heads = mesh.shape["ctx"], mesh.shape["head"]
    return jax.shard_map(
        functools.partial(per_device, shards, heads),
        mesh=mesh,
        in_specs=(P("ctx", "head"), P("ctx", "head"), P("ctx", "head"), P("ctx", "head", None)),
        out_specs=P(("ctx", "head"), None),
        check_vma=False,
    )
```

```python
import functools
import math

import jax
import jax.numpy as jnp
from jax import lax
from jax.experimental import pallas as pl
from jax.experimental.pallas import tpu as pltpu
from jax.sharding import PartitionSpec as P

MESH = pl.DeviceIdType.MESH
HD = 128
BLK = 256
KEEP = 64
GROUP = 16
PER = 4
ITEMS = GROUP // PER
COLS = PER * BLK
WIDTH = 4
SLOTS = 16
HALF = 8
KEYS = HALF * KEEP
CHUNKS = 1 + 2 * WIDTH
TAIL = 4
BUNDLE = 4
VROWS = 144
AROWS = 136
PIECE = 64
SCALE = math.log2(math.e) / math.sqrt(HD)
LOW = -1e30


def kernel(
    shards, heads, q_hbm, k_hbm, v_hbm, kept_hbm, out_ref,
    q_ref, k_ref, v_ref, kept_ref,
    compact, kv, vt, s0, s1, p0, p1, mx, al, m_ref, acc_ref, obuf,
    load_sem, send_sem, mate_send, quarter_send, column_send, single_send, bundle_send,
    mate_recv, slot_recv, bundle_recv, out_send, out_recv, own_sem,
):
    me = lax.axis_index("ctx")
    head = lax.axis_index("head")
    rows = shards // WIDTH
    row, col = lax.div(me, WIDTH), lax.rem(me, WIDTH)
    count = jnp.where(me > 0, row + 1, 0)
    bundles = lax.div(count, BUNDLE)
    scores, probs = (s0, s1), (p0, p1)

    barrier = pltpu.get_barrier_semaphore()

    def greet(block, to_head):
        pl.semaphore_signal(barrier, inc=1, device_id=(block, to_head), device_id_type=MESH)

    def mate(step):
        return row * WIDTH + lax.rem(col + step, WIDTH)

    def loop(low, high, body):
        def run(n, carry):
            body(n)
            return carry

        lax.fori_loop(low, high, run, 0)

    loop(0, row, lambda r: greet(r * WIDTH + col, head))
    for step in range(1, WIDTH):
        greet(mate(step), head)
    for step in range(1, heads):
        greet(me, lax.rem(head + step, heads))

    loads = [
        pltpu.make_async_copy(src, dst, load_sem.at[n])
        for n, (src, dst) in enumerate(
            ((kept_hbm, kept_ref), (k_hbm, k_ref), (v_hbm, v_ref), (q_hbm, q_ref))
        )
    ]
    for load in loads:
        load.start()
    for load in loads[:3]:
        load.wait()

    chosen = (
        lax.broadcasted_iota(jnp.int32, (BLK, KEEP), 0) == kept_ref[...]
    ).astype(jnp.bfloat16)
    for part, ref in ((0, k_ref), (HD, v_ref)):
        picked = lax.dot_general(
            chosen, ref[...], (((0,), (0,)), ((), ())), preferred_element_type=jnp.float32
        )
        compact[:, part : part + HD] = picked.astype(jnp.bfloat16)
    for n in range(BLK // KEEP):
        kv[0, n, :, :HD] = k_ref[n * KEEP : (n + 1) * KEEP, :]
        kv[0, n, :, HD:] = v_ref[n * KEEP : (n + 1) * KEEP, :]

    pl.semaphore_wait(barrier, rows - 1 - row + WIDTH - 1 + heads - 1)

    def remote(src, dst, send, recv, block):
        return pltpu.make_async_remote_copy(
            src_ref=src, dst_ref=dst, send_sem=send, recv_sem=recv,
            device_id=(block, head), device_id_type=MESH,
        )

    def slot_ref(c, s):
        return kv.at[1 + 2 * c + lax.div(s, HALF), lax.rem(s, HALF)]

    def bundle_ref(c, g):
        per = HALF // BUNDLE
        return kv.at[1 + 2 * c + lax.div(g, per), pl.ds(BUNDLE * lax.rem(g, per), BUNDLE)]

    def block_copy(r):
        return remote(
            compact, slot_ref(col, row + 1), send_sem.at[r], slot_recv.at[col, row + 1],
            r * WIDTH + col,
        )

    def mate_copy(c):
        return remote(
            compact, kv.at[0, 4 + col], mate_send.at[c], mate_recv.at[col], row * WIDTH + c
        )

    def quarter_copy(c):
        return remote(
            kv.at[0, c], slot_ref(c, 0), quarter_send.at[c], slot_recv.at[c, 0], c
        )

    def column_copy(source, r):
        return remote(
            source, slot_ref(col, 0), column_send.at[r], slot_recv.at[col, 0], r * WIDTH + col
        )

    loop(col + 1, WIDTH, lambda c: mate_copy(c).start())

    @pl.when(me == 0)
    def _():
        for c in range(1, WIDTH):
            quarter_copy(c).start()

    loop(0, rows - 1 - row, lambda n: block_copy(rows - 1 - n).start())

    filler = jnp.concatenate(
        [jnp.broadcast_to(k_ref[0:1, :], (KEEP, HD)), jnp.zeros((KEEP, HD), jnp.bfloat16)], axis=1
    )

    def fill_mate(c):
        kv[0, 4 + c] = filler

    def fill_slot(s):
        for c in range(WIDTH):
            kv[1 + 2 * c + lax.div(s, HALF), lax.rem(s, HALF)] = filler

    loop(col, WIDTH, fill_mate)
    loop(count, SLOTS, fill_slot)

    def wait_slot(c, s):
        pltpu.make_async_copy(compact, slot_ref(c, s), slot_recv.at[c, s]).wait()

    def single_copy(s, step):
        return remote(
            slot_ref(col, s), slot_ref(col, s), single_send.at[s, step - 1], slot_recv.at[col, s],
            mate(step),
        )

    def bundle_copy(g, step):
        return remote(
            bundle_ref(col, g), bundle_ref(col, g), bundle_send.at[g, step - 1],
            bundle_recv.at[col, g], mate(step),
        )

    def to_mates(copy, do):
        for step in (1, 3, 2):
            do(copy(step))

    def start(copy):
        copy.start()

    def zero_copy(step):
        return remote(
            kv.at[0, 0], slot_ref(0, 0), single_send.at[0, step - 1], slot_recv.at[0, 0], mate(step)
        )

    def first_copies(do):
        @pl.when(me == 0)
        def _():
            loop(1, rows, lambda r: do(column_copy(kv.at[0, 0], rows - r)))
            to_mates(zero_copy, do)

        @pl.when(jnp.logical_and(row == 0, me > 0))
        def _():
            loop(1, rows, lambda r: do(column_copy(slot_ref(col, 0), rows - r)))
            for step in (1, 3, 2):
                pl.when(mate(step) > 0)(lambda: do(single_copy(0, step)))

    @pl.when(jnp.logical_and(row == 0, me > 0))
    def _():
        wait_slot(col, 0)

    first_copies(start)

    def relay_singles():
        def one(n):
            slot = count - 1 - n
            wait_slot(col, slot)
            to_mates(functools.partial(single_copy, slot), start)

        pl.when(row > 0)(lambda: loop(0, count - BUNDLE * bundles, one))

    def relay_bundle(g):
        @pl.when(g < bundles)
        def _():
            for b in range(BUNDLE):
                wait_slot(col, BUNDLE * g + b)
            to_mates(functools.partial(bundle_copy, g), start)

    def wait_relayed(c, half):
        def many(g):
            pltpu.make_async_copy(bundle_ref(c, g), bundle_ref(c, g), bundle_recv.at[c, g]).wait()

        low = jnp.maximum(BUNDLE * bundles, HALF * half)
        loop(low, jnp.minimum(count, HALF * half + HALF), lambda s: wait_slot(c, s))
        loop(2 * half, jnp.minimum(bundles, 2 * half + 2), many)

    deep = (count > HALF).astype(jnp.int32)

    def place(p):
        k = lax.div(p - 1, 1 + deep)
        step = k + (k == 2).astype(jnp.int32) - (k == 3).astype(jnp.int32)
        half = deep * (1 - lax.rem(p - 1, 2))
        return lax.rem(col + step, WIDTH), half

    def chunk_of(p):
        c, half = place(p)
        return jnp.where(p > 0, 1 + 2 * c + half, 0)

    def load_values(chunk, limit):
        vt[chunk, 0:HD] = kv[chunk].reshape(KEYS, 2 * HD)[:, HD:].T
        valid = lax.broadcasted_iota(jnp.int32, (VROWS - HD, KEYS), 1) < limit * KEEP
        vt[chunk, HD:VROWS] = valid.astype(jnp.bfloat16)

    def load_chunk(p):
        c, half = place(p)
        pl.when(c != col)(lambda: wait_relayed(c, half))
        load_values(1 + 2 * c + half, count - HALF * half)

    chunks = 1 + WIDTH * (1 + deep)
    major = ITEMS * (chunks - TAIL)
    total = ITEMS * chunks

    def walk(t):
        late = t - major
        p = jnp.where(late < 0, lax.div(t, ITEMS), chunks - TAIL + lax.rem(late, TAIL))
        item = jnp.where(late < 0, lax.rem(t, ITEMS), lax.div(late, TAIL))
        return p, item

    def where(t):
        p, item = walk(t)
        return chunk_of(p), item

    def score(chunk, item, slot, own=False):
        keys = kv[chunk].reshape(KEYS, 2 * HD)[:, :HD]
        peaks = {}

        def part(j):
            q = q_ref[:, pl.ds(pl.multiple_of((item * PER + j) * HD, HD), HD)]
            s = SCALE * lax.dot_general(
                keys, q, (((1,), (1,)), ((), ())), preferred_element_type=jnp.float32
            )
            if own:
                key = lax.broadcasted_iota(jnp.int32, (BLK, BLK), 0)
                pos = lax.broadcasted_iota(jnp.int32, (BLK, BLK), 1)
                s = jnp.concatenate([jnp.where(key <= pos, s[:BLK], LOW), s[BLK:]], axis=0)
            scores[slot][:, j * BLK : (j + 1) * BLK] = s
            peaks[j] = s.reshape(KEYS // 8, 8, BLK).max(axis=0)

        def finish():
            for j in range(PER):
                peak = peaks[j].max(axis=0, keepdims=True)
                mx[slot, :, j * BLK : (j + 1) * BLK] = jnp.broadcast_to(peak, (8, BLK))

        return [functools.partial(part, j) for j in range(PER)], finish

    def weigh(item, slot, own=False):
        peak = mx[slot]
        if not own:
            before = m_ref[item]
            peak = jnp.maximum(before, peak)
            al[slot] = jnp.exp2(before - peak)
        m_ref[item] = peak

        def part(o):
            d = scores[slot][o : o + PIECE] - peak[0:1]
            probs[slot][o : o + PIECE] = jnp.exp2(d).astype(jnp.bfloat16)

        return [functools.partial(part, o) for o in range(0, KEYS, PIECE)]

    def mix(chunk, item, slot, own=False):
        def part(j):
            here = slice(j * BLK, (j + 1) * BLK)
            pv = jnp.dot(vt[chunk], probs[slot][:, here], preferred_element_type=jnp.float32)
            pv = pv[:AROWS]
            if not own:
                pv = acc_ref[item, :, here] * al[slot, 0:1, here] + pv
            acc_ref[item, :, here] = pv

        return [functools.partial(part, j) for j in range(PER)]

    def together(a, b, c):
        parts = []
        for order, group in enumerate((a, b, c)):
            for n, part in enumerate(group):
                parts.append(((n + 0.5) / len(group), order, part))
        for _, _, part in sorted(parts, key=lambda x: x[:2]):
            part()

    share = BLK // heads

    def out_columns(item):
        return pl.ds(pl.multiple_of((head * GROUP + item * PER) * HD, HD), PER * HD)

    def out_copy(item, step):
        peer = lax.rem(head + step, heads)
        return pltpu.make_async_remote_copy(
            src_ref=obuf.at[item, pl.ds(pl.multiple_of(peer * share, share), share)],
            dst_ref=out_ref.at[:, out_columns(item)],
            send_sem=out_send.at[item, step - 1],
            recv_sem=out_recv.at[item, step - 1],
            device_id=(me, peer),
            device_id_type=MESH,
        )

    def own_copy(item):
        return pltpu.make_async_copy(
            obuf.at[item, pl.ds(pl.multiple_of(head * share, share), share)],
            out_ref.at[:, out_columns(item)],
            own_sem.at[item],
        )

    def emit(item):
        for j in range(PER):
            a = acc_ref[item, :, j * BLK : (j + 1) * BLK]
            o = (a[:HD] / a[HD : HD + 1]).T.astype(jnp.bfloat16)
            obuf[item, :, j * HD : (j + 1) * HD] = o
        for step in range(1, heads):
            out_copy(item, step).start()
        own_copy(item).start()

    loads[3].wait()
    loop(0, col, lambda c: pltpu.make_async_copy(compact, kv.at[0, 4 + c], mate_recv.at[c]).wait())
    load_values(0, 4 + col)
    for t in range(ITEMS):
        a, finish = score(0, t, t % 2, own=True)
        b = weigh(t - 1, (t - 1) % 2, own=True) if t > 0 else []
        c = mix(0, t - 2, t % 2, own=True) if t > 1 else []
        together(a, b, c)
        finish()

    def pair(t, first=False):
        for n in range(2):
            p, item = walk(t + n + 2)
            pl.when(item == 0)(functools.partial(load_chunk, p))

            def step(n=n):
                a, finish = score(*where(t + n + 2), n)
                b = weigh(where(t + n + 1)[1], 1 - n, own=first and n == 0)
                c = mix(*where(t + n), n, own=first)
                together(a, b, c)
                finish()

            pl.when(t < total)(step)

    relay_singles()
    relay_bundle(3)
    relay_bundle(2)

    @pl.when(deep == 0)
    def _():
        relay_bundle(1)
        relay_bundle(0)

    pair(jnp.int32(ITEMS - 2), True)

    def body(n):
        t = 2 * n
        pl.when(jnp.logical_and(deep == 1, t == 4))(lambda: relay_bundle(1))
        pl.when(jnp.logical_and(deep == 1, t == 6))(lambda: relay_bundle(0))
        pair(t)
        done = t + 2 - major

        @pl.when(jnp.logical_and(done > 0, lax.rem(done, TAIL) == 0))
        def _():
            emit(lax.div(done, TAIL) - 1)

    loop(ITEMS // 2, lax.div(total, 2) - 1, body)
    together([], weigh(ITEMS - 1, 1), mix(*where(total - 2), 0))
    together([], [], mix(*where(total - 1), 1))
    emit(ITEMS - 1)

    def sent(copy):
        copy.wait_send()

    loop(col + 1, WIDTH, lambda c: sent(mate_copy(c)))

    @pl.when(me == 0)
    def _():
        for c in range(1, WIDTH):
            sent(quarter_copy(c))

    loop(row + 1, rows, lambda r: sent(block_copy(r)))
    first_copies(sent)

    @pl.when(row > 0)
    def _():
        loop(BUNDLE * bundles, count, lambda s: to_mates(functools.partial(single_copy, s), sent))
        loop(0, bundles, lambda g: to_mates(functools.partial(bundle_copy, g), sent))

    for item in range(ITEMS):
        own_copy(item).wait()
        for step in range(1, heads):
            out_copy(item, step).wait()


def per_device(shards, heads, query_rows, key_rows, value_rows, kept_rows):
    rows, depth = BLK // heads, shards // WIDTH
    f32, bf16, dma = jnp.float32, jnp.bfloat16, pltpu.SemaphoreType.DMA
    return pl.pallas_call(
        functools.partial(kernel, shards, heads),
        out_shape=jax.ShapeDtypeStruct((rows, heads * GROUP * HD), bf16),
        in_specs=[pl.BlockSpec(memory_space=pl.ANY)] * 4,
        out_specs=pl.BlockSpec(memory_space=pl.ANY),
        scratch_shapes=[
            pltpu.VMEM((BLK, GROUP * HD), bf16),
            pltpu.VMEM((BLK, HD), bf16),
            pltpu.VMEM((BLK, HD), bf16),
            pltpu.VMEM((1, KEEP), jnp.int32),
            pltpu.VMEM((KEEP, 2 * HD), bf16),
            pltpu.VMEM((CHUNKS, HALF, KEEP, 2 * HD), bf16),
            pltpu.VMEM((CHUNKS, VROWS, KEYS), bf16),
            pltpu.VMEM((KEYS, COLS), f32),
            pltpu.VMEM((KEYS, COLS), f32),
            pltpu.VMEM((KEYS, COLS), bf16),
            pltpu.VMEM((KEYS, COLS), bf16),
            pltpu.VMEM((2, 8, COLS), f32),
            pltpu.VMEM((2, 8, COLS), f32),
            pltpu.VMEM((ITEMS, 8, COLS), f32),
            pltpu.VMEM((ITEMS, AROWS, COLS), f32),
            pltpu.VMEM((ITEMS, BLK, PER * HD), bf16),
            dma((4,)),
            dma((depth,)),
            dma((WIDTH,)),
            dma((WIDTH,)),
            dma((depth,)),
            dma((SLOTS, WIDTH - 1)),
            dma((SLOTS // BUNDLE, WIDTH - 1)),
            dma((WIDTH,)),
            dma((WIDTH, SLOTS)),
            dma((WIDTH, SLOTS // BUNDLE)),
            dma((ITEMS, heads - 1)),
            dma((ITEMS, heads - 1)),
            dma((ITEMS,)),
        ],
        compiler_params=pltpu.CompilerParams(
            collective_id=0, has_side_effects=True, vmem_limit_bytes=48 * 2**20
        ),
    )(query_rows, key_rows, value_rows, kept_rows.reshape(1, KEEP))


def solution(mesh):
    shards, heads = mesh.shape["ctx"], mesh.shape["head"]
    return jax.shard_map(
        functools.partial(per_device, shards, heads),
        mesh=mesh,
        in_specs=(P("ctx", "head"), P("ctx", "head"), P("ctx", "head"), P("ctx", "head", None)),
        out_specs=P(("ctx", "head"), None),
        check_vma=False,
    )
```

```python
import functools
import math

import jax
import jax.numpy as jnp
from jax import lax
from jax.experimental import pallas as pl
from jax.experimental.pallas import tpu as pltpu
from jax.sharding import PartitionSpec as P

MESH = pl.DeviceIdType.MESH
HD = 128
BLK = 256
KEEP = 64
GROUP = 16
PER = 4
ITEMS = GROUP // PER
COLS = PER * BLK
WIDTH = 4
SLOTS = 16
HALF = 8
KEYS = HALF * KEEP
CHUNKS = 1 + 2 * WIDTH
TAIL = 4
BUNDLE = 4
VROWS = 144
AROWS = 136
PIECE = 64
SCALE = math.log2(math.e) / math.sqrt(HD)
LOW = -1e30


def kernel(
    shards, heads, q_hbm, k_hbm, v_hbm, kept_hbm, out_ref,
    q_ref, k_ref, v_ref, kept_ref,
    compact, twin, kv, vt, s0, s1, p0, p1, mx, al, m_ref, acc_ref, obuf,
    load_sem, send_sem, mate_send, quarter_send, column_send, single_send, bundle_send, twin_send, along_send,
    twin_recv, mate_recv, slot_recv, bundle_recv, out_send, out_recv, own_sem,
):
    me = lax.axis_index("ctx")
    head = lax.axis_index("head")
    rows = shards // WIDTH
    row, col = lax.div(me, WIDTH), lax.rem(me, WIDTH)
    count = jnp.where(me > 0, row + 1, 0)
    bundles = lax.div(count, BUNDLE)
    deep = (count > HALF).astype(jnp.int32)
    scores, probs = (s0, s1), (p0, p1)

    barrier = pltpu.get_barrier_semaphore()

    def greet(block, to_head):
        pl.semaphore_signal(barrier, inc=1, device_id=(block, to_head), device_id_type=MESH)

    def mate(step):
        return row * WIDTH + lax.rem(col + step, WIDTH)

    def loop(low, high, body):
        def run(n, carry):
            body(n)
            return carry

        lax.fori_loop(low, high, run, 0)

    loop(0, row, lambda r: greet(r * WIDTH + col, head))
    for step in range(1, WIDTH):
        greet(mate(step), head)
    for step in range(1, heads):
        greet(me, lax.rem(head + step, heads))
    middle = rows // 2
    pl.when(jnp.logical_and(row == middle, col > 0))(lambda: greet(0, head))

    loads = [
        pltpu.make_async_copy(src, dst, load_sem.at[n])
        for n, (src, dst) in enumerate(
            ((kept_hbm, kept_ref), (k_hbm, k_ref), (v_hbm, v_ref), (q_hbm, q_ref))
        )
    ]
    for load in loads:
        load.start()
    for load in loads[:3]:
        load.wait()

    chosen = (
        lax.broadcasted_iota(jnp.int32, (BLK, KEEP), 0) == kept_ref[...]
    ).astype(jnp.bfloat16)
    for part, ref in ((0, k_ref), (HD, v_ref)):
        picked = lax.dot_general(
            chosen, ref[...], (((0,), (0,)), ((), ())), preferred_element_type=jnp.float32
        )
        compact[:, part : part + HD] = picked.astype(jnp.bfloat16)
    for n in range(BLK // KEEP):
        kv[0, n, :, :HD] = k_ref[n * KEEP : (n + 1) * KEEP, :]
        kv[0, n, :, HD:] = v_ref[n * KEEP : (n + 1) * KEEP, :]

    extra = jnp.where(me == 0, WIDTH - 1, 0)
    pl.semaphore_wait(barrier, rows - 1 - row + WIDTH - 1 + heads - 1 + extra)

    def remote(src, dst, send, recv, block):
        return pltpu.make_async_remote_copy(
            src_ref=src, dst_ref=dst, send_sem=send, recv_sem=recv,
            device_id=(block, head), device_id_type=MESH,
        )

    def slot_ref(c, s):
        return kv.at[1 + 2 * c + lax.div(s, HALF), lax.rem(s, HALF)]

    def bundle_ref(c, g):
        per = HALF // BUNDLE
        return kv.at[1 + 2 * c + lax.div(g, per), pl.ds(BUNDLE * lax.rem(g, per), BUNDLE)]

    def block_copy(r):
        return remote(
            compact, slot_ref(col, row + 1), send_sem.at[r], slot_recv.at[col, row + 1],
            r * WIDTH + col,
        )

    def mate_copy(c):
        return remote(
            compact, kv.at[0, 4 + col], mate_send.at[c], mate_recv.at[col], row * WIDTH + c
        )

    def quarter_copy(c, r):
        return remote(
            kv.at[0, c], slot_ref(c, 0), quarter_send.at[lax.div(r, middle), c],
            slot_recv.at[c, 0], r * WIDTH + c,
        )

    def quarters(do):
        for c in range(WIDTH):
            do(quarter_copy(c, middle))
        for c in range(1, WIDTH):
            do(quarter_copy(c, 0))

    def column_copy(source, r):
        return remote(
            source, slot_ref(col, 0), column_send.at[r], slot_recv.at[col, 0], r * WIDTH + col
        )

    loop(col + 1, WIDTH, lambda c: mate_copy(c).start())

    pl.when(me == 0)(lambda: quarters(lambda copy: copy.start()))

    opposite = lax.rem(col + 2, WIDTH)
    twins = jnp.logical_and(row >= HALF - 1, row < rows - 1)

    def twin_copy():
        return remote(compact, twin, twin_send, twin_recv, mate(2))

    def twin_along(r):
        return remote(
            twin, slot_ref(opposite, row + 1), along_send.at[r], slot_recv.at[opposite, row + 1],
            r * WIDTH + col,
        )

    pl.when(twins)(lambda: twin_copy().start())
    loop(row + 1, rows, lambda r: block_copy(r).start())

    filler = jnp.concatenate(
        [jnp.broadcast_to(k_ref[0:1, :], (KEEP, HD)), jnp.zeros((KEEP, HD), jnp.bfloat16)], axis=1
    )

    def fill_mate(c):
        kv[0, 4 + c] = filler

    def fill_slot(s):
        for c in range(WIDTH):
            kv[1 + 2 * c + lax.div(s, HALF), lax.rem(s, HALF)] = filler

    loop(col, WIDTH, fill_mate)
    loop(count, SLOTS, fill_slot)

    def wait_slot(c, s):
        pltpu.make_async_copy(compact, slot_ref(c, s), slot_recv.at[c, s]).wait()

    def single_copy(s, step):
        return remote(
            slot_ref(col, s), slot_ref(col, s), single_send.at[s, step - 1], slot_recv.at[col, s],
            mate(step),
        )

    def bundle_copy(g, step):
        return remote(
            bundle_ref(col, g), bundle_ref(col, g), bundle_send.at[g, step - 1],
            bundle_recv.at[col, g], mate(step),
        )

    def to_mates(copy, do):
        for step in (1, 3, 2):
            do(copy(step))

    def to_near(copy, do):
        for step in (1, 3):
            do(copy(step))
        pl.when(deep == 0)(lambda: do(copy(2)))

    def start(copy):
        copy.start()

    def zero_copy(step):
        return remote(
            kv.at[0, 0], slot_ref(0, 0), single_send.at[0, step - 1], slot_recv.at[0, 0], mate(step)
        )

    gives = jnp.logical_or(row == 0, row == middle)

    def first_copies(do):
        def along(source):
            loop(1, middle, lambda n: do(column_copy(source, row + middle - n)))

        pl.when(me == 0)(lambda: along(kv.at[0, 0]))
        pl.when(jnp.logical_and(gives, me > 0))(lambda: along(slot_ref(col, 0)))

        pl.when(me == 0)(lambda: to_mates(zero_copy, do))

        @pl.when(jnp.logical_and(row == 0, me > 0))
        def _():
            for step in (1, 3, 2):
                pl.when(mate(step) > 0)(lambda: do(single_copy(0, step)))

    pl.when(jnp.logical_and(gives, me > 0))(lambda: wait_slot(col, 0))
    first_copies(start)

    @pl.when(twins)
    def _():
        twin_copy().wait_recv()
        loop(row + 1, rows, lambda r: twin_along(r).start())

    def relay_singles():
        def one(n):
            slot = count - 1 - n
            wait_slot(col, slot)
            to_near(functools.partial(single_copy, slot), start)

        pl.when(row > 0)(lambda: loop(0, count - BUNDLE * bundles, one))

    def relay_bundle(g):
        @pl.when(g < bundles)
        def _():
            pl.when(jnp.logical_or(g > 0, row != middle))(lambda: wait_slot(col, BUNDLE * g))
            for b in range(1, BUNDLE):
                wait_slot(col, BUNDLE * g + b)
            (to_mates if g < HALF // BUNDLE else to_near)(functools.partial(bundle_copy, g), start)

    def wait_relayed(c, half):
        def many(g):
            pltpu.make_async_copy(bundle_ref(c, g), bundle_ref(c, g), bundle_recv.at[c, g]).wait()

        whole = jnp.where(jnp.logical_and(c == opposite, half == 1), HALF // BUNDLE, bundles)
        low = jnp.maximum(BUNDLE * whole, HALF * half)
        loop(low, jnp.minimum(count, HALF * half + HALF), lambda s: wait_slot(c, s))
        loop(2 * half, jnp.minimum(whole, 2 * half + 2), many)

    def place(p):
        own = 1 + deep
        k = lax.rem(jnp.maximum(p - 1 - own, 0), WIDTH - 1)
        step = jnp.where(p > own, 1 + 2 * (k == 1).astype(jnp.int32) + (k == 2).astype(jnp.int32), 0)
        late = jnp.logical_or(p == 1, jnp.logical_and(p > own, p < own + WIDTH))
        return lax.rem(col + step, WIDTH), deep * late.astype(jnp.int32)

    def chunk_of(p):
        c, half = place(p)
        return jnp.where(p > 0, 1 + 2 * c + half, 0)

    def load_values(chunk, limit):
        vt[chunk, 0:HD] = kv[chunk].reshape(KEYS, 2 * HD)[:, HD:].T
        valid = lax.broadcasted_iota(jnp.int32, (VROWS - HD, KEYS), 1) < limit * KEEP
        vt[chunk, HD:VROWS] = valid.astype(jnp.bfloat16)

    def load_chunk(p):
        c, half = place(p)
        pl.when(c != col)(lambda: wait_relayed(c, half))
        load_values(1 + 2 * c + half, count - HALF * half)

    chunks = 1 + WIDTH * (1 + deep)
    major = ITEMS * (chunks - TAIL)
    total = ITEMS * chunks

    def walk(t):
        late = t - major
        p = jnp.where(late < 0, lax.div(t, ITEMS), chunks - TAIL + lax.rem(late, TAIL))
        item = jnp.where(late < 0, lax.rem(t, ITEMS), lax.div(late, TAIL))
        return p, item

    def where(t):
        p, item = walk(t)
        return chunk_of(p), item

    def score(chunk, item, slot, own=False):
        keys = kv[chunk].reshape(KEYS, 2 * HD)[:, :HD]
        peaks = {}

        def part(j):
            q = q_ref[:, pl.ds(pl.multiple_of((item * PER + j) * HD, HD), HD)]
            s = SCALE * lax.dot_general(
                keys, q, (((1,), (1,)), ((), ())), preferred_element_type=jnp.float32
            )
            if own:
                key = lax.broadcasted_iota(jnp.int32, (BLK, BLK), 0)
                pos = lax.broadcasted_iota(jnp.int32, (BLK, BLK), 1)
                s = jnp.concatenate([jnp.where(key <= pos, s[:BLK], LOW), s[BLK:]], axis=0)
            scores[slot][:, j * BLK : (j + 1) * BLK] = s
            peaks[j] = s.reshape(KEYS // 8, 8, BLK).max(axis=0)

        def finish():
            for j in range(PER):
                peak = peaks[j].max(axis=0, keepdims=True)
                mx[slot, :, j * BLK : (j + 1) * BLK] = jnp.broadcast_to(peak, (8, BLK))

        return [functools.partial(part, j) for j in range(PER)], finish

    def weigh(item, slot, own=False):
        peak = mx[slot]
        if not own:
            before = m_ref[item]
            peak = jnp.maximum(before, peak)
            al[slot] = jnp.exp2(before - peak)
        m_ref[item] = peak

        def part(o):
            d = scores[slot][o : o + PIECE] - peak[0:1]
            probs[slot][o : o + PIECE] = jnp.exp2(d).astype(jnp.bfloat16)

        return [functools.partial(part, o) for o in range(0, KEYS, PIECE)]

    def mix(chunk, item, slot, own=False):
        def part(j):
            here = slice(j * BLK, (j + 1) * BLK)
            pv = jnp.dot(vt[chunk], probs[slot][:, here], preferred_element_type=jnp.float32)
            pv = pv[:AROWS]
            if not own:
                pv = acc_ref[item, :, here] * al[slot, 0:1, here] + pv
            acc_ref[item, :, here] = pv

        return [functools.partial(part, j) for j in range(PER)]

    def together(a, b, c):
        parts = []
        for order, group in enumerate((a, b, c)):
            for n, part in enumerate(group):
                parts.append(((n + 0.5) / len(group), order, part))
        for _, _, part in sorted(parts, key=lambda x: x[:2]):
            part()

    share = BLK // heads

    def out_columns(item):
        return pl.ds(pl.multiple_of((head * GROUP + item * PER) * HD, HD), PER * HD)

    def out_copy(item, step):
        peer = lax.rem(head + step, heads)
        return pltpu.make_async_remote_copy(
            src_ref=obuf.at[item, pl.ds(pl.multiple_of(peer * share, share), share)],
            dst_ref=out_ref.at[:, out_columns(item)],
            send_sem=out_send.at[item, step - 1],
            recv_sem=out_recv.at[item, step - 1],
            device_id=(me, peer),
            device_id_type=MESH,
        )

    def own_copy(item):
        return pltpu.make_async_copy(
            obuf.at[item, pl.ds(pl.multiple_of(head * share, share), share)],
            out_ref.at[:, out_columns(item)],
            own_sem.at[item],
        )

    def emit(item):
        for j in range(PER):
            a = acc_ref[item, :, j * BLK : (j + 1) * BLK]
            o = (a[:HD] / a[HD : HD + 1]).T.astype(jnp.bfloat16)
            obuf[item, :, j * HD : (j + 1) * HD] = o
        for step in range(1, heads):
            out_copy(item, step).start()
        own_copy(item).start()

    loads[3].wait()
    loop(0, col, lambda c: pltpu.make_async_copy(compact, kv.at[0, 4 + c], mate_recv.at[c]).wait())
    load_values(0, 4 + col)
    for t in range(ITEMS):
        a, finish = score(0, t, t % 2, own=True)
        b = weigh(t - 1, (t - 1) % 2, own=True) if t > 0 else []
        c = mix(0, t - 2, t % 2, own=True) if t > 1 else []
        together(a, b, c)
        finish()

    def pair(t, first=False):
        for n in range(2):
            p, item = walk(t + n + 2)
            pl.when(item == 0)(functools.partial(load_chunk, p))

            def step(n=n):
                a, finish = score(*where(t + n + 2), n)
                b = weigh(where(t + n + 1)[1], 1 - n, own=first and n == 0)
                c = mix(*where(t + n), n, own=first)
                together(a, b, c)
                finish()

            pl.when(t < total)(step)

    relay_singles()
    relay_bundle(3)
    relay_bundle(2)

    @pl.when(deep == 0)
    def _():
        relay_bundle(1)
        relay_bundle(0)

    pair(jnp.int32(ITEMS - 2), True)

    def body(n):
        t = 2 * n
        pl.when(jnp.logical_and(deep == 1, t == 4))(lambda: relay_bundle(1))
        pl.when(jnp.logical_and(deep == 1, t == 6))(lambda: relay_bundle(0))
        pair(t)
        done = t + 2 - major

        @pl.when(jnp.logical_and(done > 0, lax.rem(done, TAIL) == 0))
        def _():
            emit(lax.div(done, TAIL) - 1)

    loop(ITEMS // 2, lax.div(total, 2) - 1, body)
    together([], weigh(ITEMS - 1, 1), mix(*where(total - 2), 0))
    together([], [], mix(*where(total - 1), 1))
    emit(ITEMS - 1)

    def sent(copy):
        copy.wait_send()

    loop(col + 1, WIDTH, lambda c: sent(mate_copy(c)))

    pl.when(me == 0)(lambda: quarters(sent))

    loop(row + 1, rows, lambda r: sent(block_copy(r)))
    first_copies(sent)

    @pl.when(row > 0)
    def _():
        loop(BUNDLE * bundles, count, lambda s: to_near(functools.partial(single_copy, s), sent))
        early = jnp.minimum(bundles, HALF // BUNDLE)
        loop(0, early, lambda g: to_mates(functools.partial(bundle_copy, g), sent))
        loop(early, bundles, lambda g: to_near(functools.partial(bundle_copy, g), sent))

    @pl.when(twins)
    def _():
        twin_copy().wait_send()
        loop(row + 1, rows, lambda r: twin_along(r).wait_send())

    for item in range(ITEMS):
        own_copy(item).wait()
        for step in range(1, heads):
            out_copy(item, step).wait()


def per_device(shards, heads, query_rows, key_rows, value_rows, kept_rows):
    rows, depth = BLK // heads, shards // WIDTH
    f32, bf16, dma = jnp.float32, jnp.bfloat16, pltpu.SemaphoreType.DMA
    return pl.pallas_call(
        functools.partial(kernel, shards, heads),
        out_shape=jax.ShapeDtypeStruct((rows, heads * GROUP * HD), bf16),
        in_specs=[pl.BlockSpec(memory_space=pl.ANY)] * 4,
        out_specs=pl.BlockSpec(memory_space=pl.ANY),
        scratch_shapes=[
            pltpu.VMEM((BLK, GROUP * HD), bf16),
            pltpu.VMEM((BLK, HD), bf16),
            pltpu.VMEM((BLK, HD), bf16),
            pltpu.VMEM((1, KEEP), jnp.int32),
            pltpu.VMEM((KEEP, 2 * HD), bf16),
            pltpu.VMEM((KEEP, 2 * HD), bf16),
            pltpu.VMEM((CHUNKS, HALF, KEEP, 2 * HD), bf16),
            pltpu.VMEM((CHUNKS, VROWS, KEYS), bf16),
            pltpu.VMEM((KEYS, COLS), f32),
            pltpu.VMEM((KEYS, COLS), f32),
            pltpu.VMEM((KEYS, COLS), bf16),
            pltpu.VMEM((KEYS, COLS), bf16),
            pltpu.VMEM((2, 8, COLS), f32),
            pltpu.VMEM((2, 8, COLS), f32),
            pltpu.VMEM((ITEMS, 8, COLS), f32),
            pltpu.VMEM((ITEMS, AROWS, COLS), f32),
            pltpu.VMEM((ITEMS, BLK, PER * HD), bf16),
            dma((4,)),
            dma((depth,)),
            dma((WIDTH,)),
            dma((2, WIDTH)),
            dma((depth,)),
            dma((SLOTS, WIDTH - 1)),
            dma((SLOTS // BUNDLE, WIDTH - 1)),
            dma,
            dma((depth,)),
            dma,
            dma((WIDTH,)),
            dma((WIDTH, SLOTS)),
            dma((WIDTH, SLOTS // BUNDLE)),
            dma((ITEMS, heads - 1)),
            dma((ITEMS, heads - 1)),
            dma((ITEMS,)),
        ],
        compiler_params=pltpu.CompilerParams(
            collective_id=0, has_side_effects=True, vmem_limit_bytes=48 * 2**20
        ),
    )(query_rows, key_rows, value_rows, kept_rows.reshape(1, KEEP))


def solution(mesh):
    shards, heads = mesh.shape["ctx"], mesh.shape["head"]
    return jax.shard_map(
        functools.partial(per_device, shards, heads),
        mesh=mesh,
        in_specs=(P("ctx", "head"), P("ctx", "head"), P("ctx", "head"), P("ctx", "head", None)),
        out_specs=P(("ctx", "head"), None),
        check_vma=False,
    )
```

```python
import functools
import math

import jax
import jax.numpy as jnp
from jax import lax
from jax.experimental import pallas as pl
from jax.experimental.pallas import tpu as pltpu
from jax.sharding import PartitionSpec as P

MESH = pl.DeviceIdType.MESH
HD = 128
BLK = 256
KEEP = 64
GROUP = 16
PER = 4
ITEMS = GROUP // PER
COLS = PER * BLK
WIDTH = 4
SLOTS = 16
HALF = 8
KEYS = HALF * KEEP
CHUNKS = 1 + 2 * WIDTH
TAIL = 4
BUNDLE = 4
VROWS = 144
AROWS = 136
PIECE = 64
SCALE = math.log2(math.e) / math.sqrt(HD)
LOW = -1e30


def kernel(
    shards, heads, q_hbm, k_hbm, v_hbm, kept_hbm, out_ref,
    q_ref, k_ref, v_ref, kept_ref,
    compact, twin, kv, vt, s0, s1, p0, p1, mx, al, m_ref, acc_ref, obuf,
    load_sem, send_sem, mate_send, quarter_send, column_send, single_send, bundle_send, twin_send, along_send,
    twin_recv, mate_recv, slot_recv, bundle_recv, out_send, out_recv, own_sem,
):
    me = lax.axis_index("ctx")
    head = lax.axis_index("head")
    rows = shards // WIDTH
    row, col = lax.div(me, WIDTH), lax.rem(me, WIDTH)
    count = jnp.where(me > 0, row + 1, 0)
    bundles = lax.div(count, BUNDLE)
    deep = (count > HALF).astype(jnp.int32)
    scores, probs = (s0, s1), (p0, p1)

    barrier = pltpu.get_barrier_semaphore()

    def greet(block, to_head):
        pl.semaphore_signal(barrier, inc=1, device_id=(block, to_head), device_id_type=MESH)

    def mate(step):
        return row * WIDTH + lax.rem(col + step, WIDTH)

    def loop(low, high, body):
        def run(n, carry):
            body(n)
            return carry

        lax.fori_loop(low, high, run, 0)

    loop(0, row, lambda r: greet(r * WIDTH + col, head))
    for step in range(1, WIDTH):
        greet(mate(step), head)
    for step in range(1, heads):
        greet(me, lax.rem(head + step, heads))
    middle = rows // 2
    pl.when(jnp.logical_and(row == middle, col > 0))(lambda: greet(0, head))

    loads = [
        pltpu.make_async_copy(src, dst, load_sem.at[n])
        for n, (src, dst) in enumerate(
            ((kept_hbm, kept_ref), (k_hbm, k_ref), (v_hbm, v_ref), (q_hbm, q_ref))
        )
    ]
    for load in loads:
        load.start()
    for load in loads[:3]:
        load.wait()

    chosen = (
        lax.broadcasted_iota(jnp.int32, (BLK, KEEP), 0) == kept_ref[...]
    ).astype(jnp.bfloat16)
    for part, ref in ((0, k_ref), (HD, v_ref)):
        picked = lax.dot_general(
            chosen, ref[...], (((0,), (0,)), ((), ())), preferred_element_type=jnp.float32
        )
        compact[:, part : part + HD] = picked.astype(jnp.bfloat16)
    for n in range(BLK // KEEP):
        kv[0, n, :, :HD] = k_ref[n * KEEP : (n + 1) * KEEP, :]
        kv[0, n, :, HD:] = v_ref[n * KEEP : (n + 1) * KEEP, :]

    extra = jnp.where(me == 0, WIDTH - 1, 0)
    pl.semaphore_wait(barrier, rows - 1 - row + WIDTH - 1 + heads - 1 + extra)

    def remote(src, dst, send, recv, block):
        return pltpu.make_async_remote_copy(
            src_ref=src, dst_ref=dst, send_sem=send, recv_sem=recv,
            device_id=(block, head), device_id_type=MESH,
        )

    def slot_ref(c, s):
        return kv.at[1 + 2 * c + lax.div(s, HALF), lax.rem(s, HALF)]

    def bundle_ref(c, g):
        per = HALF // BUNDLE
        return kv.at[1 + 2 * c + lax.div(g, per), pl.ds(BUNDLE * lax.rem(g, per), BUNDLE)]

    def block_copy(r):
        return remote(
            compact, slot_ref(col, row + 1), send_sem.at[r], slot_recv.at[col, row + 1],
            r * WIDTH + col,
        )

    def mate_copy(c):
        return remote(
            compact, kv.at[0, 4 + col], mate_send.at[c], mate_recv.at[col], row * WIDTH + c
        )

    def quarter_copy(c, r):
        return remote(
            kv.at[0, c], slot_ref(c, 0), quarter_send.at[lax.div(r, middle), c],
            slot_recv.at[c, 0], r * WIDTH + c,
        )

    def quarters(do):
        for c in range(WIDTH):
            do(quarter_copy(c, middle))
        for c in range(1, WIDTH):
            do(quarter_copy(c, 0))

    def column_copy(source, r):
        return remote(
            source, slot_ref(col, 0), column_send.at[r], slot_recv.at[col, 0], r * WIDTH + col
        )

    loop(col + 1, WIDTH, lambda c: mate_copy(c).start())

    pl.when(me == 0)(lambda: quarters(lambda copy: copy.start()))

    opposite = lax.rem(col + 2, WIDTH)
    twins = jnp.logical_and(row >= HALF - 1, row < rows - 1)

    def twin_copy():
        return remote(compact, twin, twin_send, twin_recv, mate(2))

    def twin_along(r):
        return remote(
            twin, slot_ref(opposite, row + 1), along_send.at[r], slot_recv.at[opposite, row + 1],
            r * WIDTH + col,
        )

    def target(n):
        plain = rows - 1 - n
        turned = jnp.where(n == 2, rows - 1, jnp.where(n < 2, plain - 1, plain))
        return jnp.where(row < rows - 3, turned, plain)

    pl.when(twins)(lambda: twin_copy().start())
    loop(0, rows - 1 - row, lambda n: block_copy(target(n)).start())

    filler = jnp.concatenate(
        [jnp.broadcast_to(k_ref[0:1, :], (KEEP, HD)), jnp.zeros((KEEP, HD), jnp.bfloat16)], axis=1
    )

    def fill_mate(c):
        kv[0, 4 + c] = filler

    def fill_slot(s):
        for c in range(WIDTH):
            kv[1 + 2 * c + lax.div(s, HALF), lax.rem(s, HALF)] = filler

    loop(col, WIDTH, fill_mate)
    loop(count, SLOTS, fill_slot)

    def wait_slot(c, s):
        pltpu.make_async_copy(compact, slot_ref(c, s), slot_recv.at[c, s]).wait()

    def single_copy(s, step):
        return remote(
            slot_ref(col, s), slot_ref(col, s), single_send.at[s, step - 1], slot_recv.at[col, s],
            mate(step),
        )

    def bundle_copy(g, step):
        return remote(
            bundle_ref(col, g), bundle_ref(col, g), bundle_send.at[g, step - 1],
            bundle_recv.at[col, g], mate(step),
        )

    def to_mates(copy, do):
        for step in (1, 3, 2):
            do(copy(step))

    def to_near(copy, do):
        for step in (1, 3):
            do(copy(step))
        pl.when(deep == 0)(lambda: do(copy(2)))

    def start(copy):
        copy.start()

    def zero_copy(step):
        return remote(
            kv.at[0, 0], slot_ref(0, 0), single_send.at[0, step - 1], slot_recv.at[0, 0], mate(step)
        )

    gives = jnp.logical_or(row == 0, row == middle)

    def first_copies(do):
        def along(source):
            loop(1, middle, lambda n: do(column_copy(source, row + middle - n)))

        pl.when(me == 0)(lambda: along(kv.at[0, 0]))
        pl.when(jnp.logical_and(gives, me > 0))(lambda: along(slot_ref(col, 0)))

        pl.when(me == 0)(lambda: to_mates(zero_copy, do))

        @pl.when(jnp.logical_and(row == 0, me > 0))
        def _():
            for step in (1, 3, 2):
                pl.when(mate(step) > 0)(lambda: do(single_copy(0, step)))

    pl.when(jnp.logical_and(gives, me > 0))(lambda: wait_slot(col, 0))
    first_copies(start)

    @pl.when(twins)
    def _():
        twin_copy().wait_recv()
        loop(row + 1, rows, lambda r: twin_along(r).start())

    def relay_singles():
        def one(n):
            slot = count - 1 - n
            wait_slot(col, slot)
            to_near(functools.partial(single_copy, slot), start)

        pl.when(row > 0)(lambda: loop(0, count - BUNDLE * bundles, one))

    def relay_bundle(g):
        @pl.when(g < bundles)
        def _():
            pl.when(jnp.logical_or(g > 0, row != middle))(lambda: wait_slot(col, BUNDLE * g))
            for b in range(1, BUNDLE):
                wait_slot(col, BUNDLE * g + b)
            (to_mates if g < HALF // BUNDLE else to_near)(functools.partial(bundle_copy, g), start)

    def wait_relayed(c, half):
        def many(g):
            pltpu.make_async_copy(bundle_ref(c, g), bundle_ref(c, g), bundle_recv.at[c, g]).wait()

        whole = jnp.where(jnp.logical_and(c == opposite, half == 1), HALF // BUNDLE, bundles)
        low = jnp.maximum(BUNDLE * whole, HALF * half)
        loop(low, jnp.minimum(count, HALF * half + HALF), lambda s: wait_slot(c, s))
        loop(2 * half, jnp.minimum(whole, 2 * half + 2), many)

    def place(p):
        own = 1 + deep
        k = lax.rem(jnp.maximum(p - 1 - own, 0), WIDTH - 1)
        step = jnp.where(p > own, 1 + 2 * (k == 1).astype(jnp.int32) + (k == 2).astype(jnp.int32), 0)
        late = jnp.logical_or(p == 1, jnp.logical_and(p > own, p < own + WIDTH))
        return lax.rem(col + step, WIDTH), deep * late.astype(jnp.int32)

    def chunk_of(p):
        c, half = place(p)
        return jnp.where(p > 0, 1 + 2 * c + half, 0)

    def load_values(chunk, limit):
        vt[chunk, 0:HD] = kv[chunk].reshape(KEYS, 2 * HD)[:, HD:].T
        valid = lax.broadcasted_iota(jnp.int32, (VROWS - HD, KEYS), 1) < limit * KEEP
        vt[chunk, HD:VROWS] = valid.astype(jnp.bfloat16)

    def load_chunk(p):
        c, half = place(p)
        pl.when(c != col)(lambda: wait_relayed(c, half))
        load_values(1 + 2 * c + half, count - HALF * half)

    chunks = 1 + WIDTH * (1 + deep)
    major = ITEMS * (chunks - TAIL)
    total = ITEMS * chunks

    def walk(t):
        late = t - major
        p = jnp.where(late < 0, lax.div(t, ITEMS), chunks - TAIL + lax.rem(late, TAIL))
        item = jnp.where(late < 0, lax.rem(t, ITEMS), lax.div(late, TAIL))
        return p, item

    def where(t):
        p, item = walk(t)
        return chunk_of(p), item

    def score(chunk, item, slot, own=False):
        keys = kv[chunk].reshape(KEYS, 2 * HD)[:, :HD]
        peaks = {}

        def part(j):
            q = q_ref[:, pl.ds(pl.multiple_of((item * PER + j) * HD, HD), HD)]
            s = SCALE * lax.dot_general(
                keys, q, (((1,), (1,)), ((), ())), preferred_element_type=jnp.float32
            )
            if own:
                key = lax.broadcasted_iota(jnp.int32, (BLK, BLK), 0)
                pos = lax.broadcasted_iota(jnp.int32, (BLK, BLK), 1)
                s = jnp.concatenate([jnp.where(key <= pos, s[:BLK], LOW), s[BLK:]], axis=0)
            scores[slot][:, j * BLK : (j + 1) * BLK] = s
            peaks[j] = s.reshape(KEYS // 8, 8, BLK).max(axis=0)

        def finish():
            for j in range(PER):
                peak = peaks[j].max(axis=0, keepdims=True)
                mx[slot, :, j * BLK : (j + 1) * BLK] = jnp.broadcast_to(peak, (8, BLK))

        return [functools.partial(part, j) for j in range(PER)], finish

    def weigh(item, slot, own=False):
        peak = mx[slot]
        if not own:
            before = m_ref[item]
            peak = jnp.maximum(before, peak)
            al[slot] = jnp.exp2(before - peak)
        m_ref[item] = peak

        def part(o):
            d = scores[slot][o : o + PIECE] - peak[0:1]
            probs[slot][o : o + PIECE] = jnp.exp2(d).astype(jnp.bfloat16)

        return [functools.partial(part, o) for o in range(0, KEYS, PIECE)]

    def mix(chunk, item, slot, own=False):
        def part(j):
            here = slice(j * BLK, (j + 1) * BLK)
            pv = jnp.dot(vt[chunk], probs[slot][:, here], preferred_element_type=jnp.float32)
            pv = pv[:AROWS]
            if not own:
                pv = acc_ref[item, :, here] * al[slot, 0:1, here] + pv
            acc_ref[item, :, here] = pv

        return [functools.partial(part, j) for j in range(PER)]

    def together(a, b, c):
        parts = []
        for order, group in enumerate((a, b, c)):
            for n, part in enumerate(group):
                parts.append(((n + 0.5) / len(group), order, part))
        for _, _, part in sorted(parts, key=lambda x: x[:2]):
            part()

    share = BLK // heads

    def out_columns(item):
        return pl.ds(pl.multiple_of((head * GROUP + item * PER) * HD, HD), PER * HD)

    def out_copy(item, step):
        peer = lax.rem(head + step, heads)
        return pltpu.make_async_remote_copy(
            src_ref=obuf.at[item, pl.ds(pl.multiple_of(peer * share, share), share)],
            dst_ref=out_ref.at[:, out_columns(item)],
            send_sem=out_send.at[item, step - 1],
            recv_sem=out_recv.at[item, step - 1],
            device_id=(me, peer),
            device_id_type=MESH,
        )

    def own_copy(item):
        return pltpu.make_async_copy(
            obuf.at[item, pl.ds(pl.multiple_of(head * share, share), share)],
            out_ref.at[:, out_columns(item)],
            own_sem.at[item],
        )

    def emit(item):
        for j in range(PER):
            a = acc_ref[item, :, j * BLK : (j + 1) * BLK]
            o = (a[:HD] / a[HD : HD + 1]).T.astype(jnp.bfloat16)
            obuf[item, :, j * HD : (j + 1) * HD] = o
        for step in (2, 1, 3):
            out_copy(item, step).start()
        own_copy(item).start()

    loads[3].wait()
    loop(0, col, lambda c: pltpu.make_async_copy(compact, kv.at[0, 4 + c], mate_recv.at[c]).wait())
    load_values(0, 4 + col)
    for t in range(ITEMS):
        a, finish = score(0, t, t % 2, own=True)
        b = weigh(t - 1, (t - 1) % 2, own=True) if t > 0 else []
        c = mix(0, t - 2, t % 2, own=True) if t > 1 else []
        together(a, b, c)
        finish()

    def pair(t, first=False):
        for n in range(2):
            p, item = walk(t + n + 2)
            pl.when(item == 0)(functools.partial(load_chunk, p))

            def step(n=n):
                a, finish = score(*where(t + n + 2), n)
                b = weigh(where(t + n + 1)[1], 1 - n, own=first and n == 0)
                c = mix(*where(t + n), n, own=first)
                together(a, b, c)
                finish()

            pl.when(t < total)(step)

    relay_singles()
    relay_bundle(3)
    relay_bundle(2)

    @pl.when(deep == 0)
    def _():
        relay_bundle(1)
        relay_bundle(0)

    pair(jnp.int32(ITEMS - 2), True)

    def body(n):
        t = 2 * n
        pl.when(jnp.logical_and(deep == 1, t == 4))(lambda: relay_bundle(1))
        pl.when(jnp.logical_and(deep == 1, t == 6))(lambda: relay_bundle(0))
        pair(t)
        done = t + 2 - major

        @pl.when(jnp.logical_and(done > 0, lax.rem(done, TAIL) == 0))
        def _():
            emit(lax.div(done, TAIL) - 1)

    loop(ITEMS // 2, lax.div(total, 2) - 1, body)
    together([], weigh(ITEMS - 1, 1), mix(*where(total - 2), 0))
    together([], [], mix(*where(total - 1), 1))
    emit(ITEMS - 1)

    def sent(copy):
        copy.wait_send()

    loop(col + 1, WIDTH, lambda c: sent(mate_copy(c)))

    pl.when(me == 0)(lambda: quarters(sent))

    loop(row + 1, rows, lambda r: sent(block_copy(r)))
    first_copies(sent)

    @pl.when(row > 0)
    def _():
        loop(BUNDLE * bundles, count, lambda s: to_near(functools.partial(single_copy, s), sent))
        early = jnp.minimum(bundles, HALF // BUNDLE)
        loop(0, early, lambda g: to_mates(functools.partial(bundle_copy, g), sent))
        loop(early, bundles, lambda g: to_near(functools.partial(bundle_copy, g), sent))

    @pl.when(twins)
    def _():
        twin_copy().wait_send()
        loop(row + 1, rows, lambda r: twin_along(r).wait_send())

    for item in range(ITEMS):
        own_copy(item).wait()
        for step in range(1, heads):
            out_copy(item, step).wait()


def per_device(shards, heads, query_rows, key_rows, value_rows, kept_rows):
    rows, depth = BLK // heads, shards // WIDTH
    f32, bf16, dma = jnp.float32, jnp.bfloat16, pltpu.SemaphoreType.DMA
    return pl.pallas_call(
        functools.partial(kernel, shards, heads),
        out_shape=jax.ShapeDtypeStruct((rows, heads * GROUP * HD), bf16),
        in_specs=[pl.BlockSpec(memory_space=pl.ANY)] * 4,
        out_specs=pl.BlockSpec(memory_space=pl.ANY),
        scratch_shapes=[
            pltpu.VMEM((BLK, GROUP * HD), bf16),
            pltpu.VMEM((BLK, HD), bf16),
            pltpu.VMEM((BLK, HD), bf16),
            pltpu.VMEM((1, KEEP), jnp.int32),
            pltpu.VMEM((KEEP, 2 * HD), bf16),
            pltpu.VMEM((KEEP, 2 * HD), bf16),
            pltpu.VMEM((CHUNKS, HALF, KEEP, 2 * HD), bf16),
            pltpu.VMEM((CHUNKS, VROWS, KEYS), bf16),
            pltpu.VMEM((KEYS, COLS), f32),
            pltpu.VMEM((KEYS, COLS), f32),
            pltpu.VMEM((KEYS, COLS), bf16),
            pltpu.VMEM((KEYS, COLS), bf16),
            pltpu.VMEM((2, 8, COLS), f32),
            pltpu.VMEM((2, 8, COLS), f32),
            pltpu.VMEM((ITEMS, 8, COLS), f32),
            pltpu.VMEM((ITEMS, AROWS, COLS), f32),
            pltpu.VMEM((ITEMS, BLK, PER * HD), bf16),
            dma((4,)),
            dma((depth,)),
            dma((WIDTH,)),
            dma((2, WIDTH)),
            dma((depth,)),
            dma((SLOTS, WIDTH - 1)),
            dma((SLOTS // BUNDLE, WIDTH - 1)),
            dma,
            dma((depth,)),
            dma,
            dma((WIDTH,)),
            dma((WIDTH, SLOTS)),
            dma((WIDTH, SLOTS // BUNDLE)),
            dma((ITEMS, heads - 1)),
            dma((ITEMS, heads - 1)),
            dma((ITEMS,)),
        ],
        compiler_params=pltpu.CompilerParams(
            collective_id=0, has_side_effects=True, vmem_limit_bytes=48 * 2**20
        ),
    )(query_rows, key_rows, value_rows, kept_rows.reshape(1, KEEP))


def solution(mesh):
    shards, heads = mesh.shape["ctx"], mesh.shape["head"]
    return jax.shard_map(
        functools.partial(per_device, shards, heads),
        mesh=mesh,
        in_specs=(P("ctx", "head"), P("ctx", "head"), P("ctx", "head"), P("ctx", "head", None)),
        out_specs=P(("ctx", "head"), None),
        check_vma=False,
    )
```

```python
import functools
import math

import jax
import jax.numpy as jnp
from jax import lax
from jax.experimental import pallas as pl
from jax.experimental.pallas import tpu as pltpu
from jax.sharding import PartitionSpec as P

MESH = pl.DeviceIdType.MESH
HD = 128
BLK = 256
KEEP = 64
GROUP = 16
PER = 4
ITEMS = GROUP // PER
COLS = PER * BLK
WIDTH = 4
SLOTS = 16
HALF = 8
KEYS = HALF * KEEP
CHUNKS = 1 + 2 * WIDTH
TAIL = 4
BUNDLE = 4
VROWS = 144
AROWS = 136
PIECE = 64
SCALE = math.log2(math.e) / math.sqrt(HD)
LOW = -1e30


def kernel(
    shards, heads, q_hbm, k_hbm, v_hbm, kept_hbm, out_ref,
    q_ref, k_ref, v_ref, kept_ref,
    compact, twin, kv, vt, s0, s1, p0, p1, mx, al, m_ref, acc_ref, obuf,
    load_sem, send_sem, mate_send, quarter_send, column_send, single_send, bundle_send, twin_send, along_send,
    twin_recv, mate_recv, slot_recv, bundle_recv, out_send, out_recv, own_sem,
):
    me = lax.axis_index("ctx")
    head = lax.axis_index("head")
    rows = shards // WIDTH
    row, col = lax.div(me, WIDTH), lax.rem(me, WIDTH)
    count = jnp.where(me > 0, row + 1, 0)
    bundles = lax.div(count, BUNDLE)
    deep = (count > HALF).astype(jnp.int32)
    scores, probs = (s0, s1), (p0, p1)

    barrier = pltpu.get_barrier_semaphore()

    def greet(block, to_head):
        pl.semaphore_signal(barrier, inc=1, device_id=(block, to_head), device_id_type=MESH)

    def mate(step):
        return row * WIDTH + lax.rem(col + step, WIDTH)

    def loop(low, high, body):
        def run(n, carry):
            body(n)
            return carry

        lax.fori_loop(low, high, run, 0)

    loop(0, row, lambda r: greet(r * WIDTH + col, head))
    for step in range(1, WIDTH):
        greet(mate(step), head)
    for step in range(1, heads):
        greet(me, lax.rem(head + step, heads))
    middle = rows // 2
    pl.when(jnp.logical_and(row == middle, col > 0))(lambda: greet(0, head))

    loads = [
        pltpu.make_async_copy(src, dst, load_sem.at[n])
        for n, (src, dst) in enumerate(
            ((kept_hbm, kept_ref), (k_hbm, k_ref), (v_hbm, v_ref), (q_hbm, q_ref))
        )
    ]
    for load in loads:
        load.start()
    for load in loads[:3]:
        load.wait()

    chosen = (
        lax.broadcasted_iota(jnp.int32, (BLK, KEEP), 0) == kept_ref[...]
    ).astype(jnp.bfloat16)
    for part, ref in ((0, k_ref), (HD, v_ref)):
        picked = lax.dot_general(
            chosen, ref[...], (((0,), (0,)), ((), ())), preferred_element_type=jnp.float32
        )
        compact[:, part : part + HD] = picked.astype(jnp.bfloat16)
    for n in range(BLK // KEEP):
        kv[0, n, :, :HD] = k_ref[n * KEEP : (n + 1) * KEEP, :]
        kv[0, n, :, HD:] = v_ref[n * KEEP : (n + 1) * KEEP, :]

    extra = jnp.where(me == 0, WIDTH - 1, 0)
    pl.semaphore_wait(barrier, rows - 1 - row + WIDTH - 1 + heads - 1 + extra)

    def remote(src, dst, send, recv, block):
        return pltpu.make_async_remote_copy(
            src_ref=src, dst_ref=dst, send_sem=send, recv_sem=recv,
            device_id=(block, head), device_id_type=MESH,
        )

    def slot_ref(c, s):
        return kv.at[1 + 2 * c + lax.div(s, HALF), lax.rem(s, HALF)]

    def bundle_ref(c, g):
        per = HALF // BUNDLE
        return kv.at[1 + 2 * c + lax.div(g, per), pl.ds(BUNDLE * lax.rem(g, per), BUNDLE)]

    def block_copy(r):
        return remote(
            compact, slot_ref(col, row + 1), send_sem.at[r], slot_recv.at[col, row + 1],
            r * WIDTH + col,
        )

    def mate_copy(c):
        return remote(
            compact, kv.at[0, 4 + col], mate_send.at[c], mate_recv.at[col], row * WIDTH + c
        )

    def quarter_copy(c, r):
        return remote(
            kv.at[0, c], slot_ref(c, 0), quarter_send.at[lax.div(r, middle), c],
            slot_recv.at[c, 0], r * WIDTH + c,
        )

    def quarters(do):
        for c in range(WIDTH):
            do(quarter_copy(c, middle))
        for c in range(1, WIDTH):
            do(quarter_copy(c, 0))

    def column_copy(source, r):
        return remote(
            source, slot_ref(col, 0), column_send.at[r], slot_recv.at[col, 0], r * WIDTH + col
        )

    loop(col + 1, WIDTH, lambda c: mate_copy(c).start())

    pl.when(me == 0)(lambda: quarters(lambda copy: copy.start()))

    opposite = lax.rem(col + 2, WIDTH)
    twins = jnp.logical_and(row >= BUNDLE - 1, row < rows - 1)

    def twin_copy():
        return remote(compact, twin, twin_send, twin_recv, mate(2))

    def twin_along(r):
        return remote(
            twin, slot_ref(opposite, row + 1), along_send.at[r], slot_recv.at[opposite, row + 1],
            r * WIDTH + col,
        )

    def target(n):
        plain = rows - 1 - n
        turned = jnp.where(n == 2, rows - 1, jnp.where(n < 2, plain - 1, plain))
        return jnp.where(row < rows - 3, turned, plain)

    pl.when(twins)(lambda: twin_copy().start())
    loop(0, rows - 1 - row, lambda n: block_copy(target(n)).start())

    filler = jnp.concatenate(
        [jnp.broadcast_to(k_ref[0:1, :], (KEEP, HD)), jnp.zeros((KEEP, HD), jnp.bfloat16)], axis=1
    )

    def fill_mate(c):
        kv[0, 4 + c] = filler

    def fill_slot(s):
        for c in range(WIDTH):
            kv[1 + 2 * c + lax.div(s, HALF), lax.rem(s, HALF)] = filler

    loop(col, WIDTH, fill_mate)
    loop(count, SLOTS, fill_slot)

    def wait_slot(c, s):
        pltpu.make_async_copy(compact, slot_ref(c, s), slot_recv.at[c, s]).wait()

    def single_copy(s, step):
        return remote(
            slot_ref(col, s), slot_ref(col, s), single_send.at[s, step - 1], slot_recv.at[col, s],
            mate(step),
        )

    def bundle_copy(g, step):
        return remote(
            bundle_ref(col, g), bundle_ref(col, g), bundle_send.at[g, step - 1],
            bundle_recv.at[col, g], mate(step),
        )

    def to_mates(copy, do):
        for step in (1, 3, 2):
            do(copy(step))

    def to_near(copy, do):
        for step in (1, 3):
            do(copy(step))
        pl.when(deep == 0)(lambda: do(copy(2)))

    def start(copy):
        copy.start()

    def zero_copy(step):
        return remote(
            kv.at[0, 0], slot_ref(0, 0), single_send.at[0, step - 1], slot_recv.at[0, 0], mate(step)
        )

    gives = jnp.logical_or(row == 0, row == middle)

    def first_copies(do):
        def along(source):
            loop(1, middle, lambda n: do(column_copy(source, row + middle - n)))

        pl.when(me == 0)(lambda: along(kv.at[0, 0]))
        pl.when(jnp.logical_and(gives, me > 0))(lambda: along(slot_ref(col, 0)))

        pl.when(me == 0)(lambda: to_mates(zero_copy, do))

        @pl.when(jnp.logical_and(row == 0, me > 0))
        def _():
            for step in (1, 3, 2):
                pl.when(mate(step) > 0)(lambda: do(single_copy(0, step)))

    pl.when(jnp.logical_and(gives, me > 0))(lambda: wait_slot(col, 0))
    first_copies(start)

    @pl.when(twins)
    def _():
        twin_copy().wait_recv()
        loop(jnp.maximum(row + 1, HALF), rows, lambda r: twin_along(r).start())

    def relay_singles():
        def one(n):
            slot = count - 1 - n
            wait_slot(col, slot)
            to_near(functools.partial(single_copy, slot), start)

        pl.when(row > 0)(lambda: loop(0, count - BUNDLE * bundles, one))

    def relay_bundle(g):
        @pl.when(g < bundles)
        def _():
            pl.when(jnp.logical_or(g > 0, row != middle))(lambda: wait_slot(col, BUNDLE * g))
            for b in range(1, BUNDLE):
                wait_slot(col, BUNDLE * g + b)
            (to_near if g > 0 else to_mates)(functools.partial(bundle_copy, g), start)

    def wait_relayed(c, half):
        def many(g):
            pltpu.make_async_copy(bundle_ref(c, g), bundle_ref(c, g), bundle_recv.at[c, g]).wait()

        whole = jnp.where(jnp.logical_and(c == opposite, deep == 1), 1, bundles)
        low = jnp.maximum(BUNDLE * whole, HALF * half)
        loop(low, jnp.minimum(count, HALF * half + HALF), lambda s: wait_slot(c, s))
        loop(2 * half, jnp.minimum(whole, 2 * half + 2), many)

    def place(p):
        own = 1 + deep
        k = lax.rem(jnp.maximum(p - 1 - own, 0), WIDTH - 1)
        step = jnp.where(p > own, 1 + 2 * (k == 1).astype(jnp.int32) + (k == 2).astype(jnp.int32), 0)
        late = jnp.logical_or(p == 1, jnp.logical_and(p > own, p < own + WIDTH))
        return lax.rem(col + step, WIDTH), deep * late.astype(jnp.int32)

    def chunk_of(p):
        c, half = place(p)
        return jnp.where(p > 0, 1 + 2 * c + half, 0)

    def load_values(chunk, limit):
        vt[chunk, 0:HD] = kv[chunk].reshape(KEYS, 2 * HD)[:, HD:].T
        valid = lax.broadcasted_iota(jnp.int32, (VROWS - HD, KEYS), 1) < limit * KEEP
        vt[chunk, HD:VROWS] = valid.astype(jnp.bfloat16)

    def load_chunk(p):
        c, half = place(p)
        pl.when(c != col)(lambda: wait_relayed(c, half))
        load_values(1 + 2 * c + half, count - HALF * half)

    chunks = 1 + WIDTH * (1 + deep)
    major = ITEMS * (chunks - TAIL)
    total = ITEMS * chunks

    def walk(t):
        late = t - major
        p = jnp.where(late < 0, lax.div(t, ITEMS), chunks - TAIL + lax.rem(late, TAIL))
        item = jnp.where(late < 0, lax.rem(t, ITEMS), lax.div(late, TAIL))
        return p, item

    def where(t):
        p, item = walk(t)
        return chunk_of(p), item

    def score(chunk, item, slot, own=False):
        keys = kv[chunk].reshape(KEYS, 2 * HD)[:, :HD]
        peaks = {}

        def part(j):
            q = q_ref[:, pl.ds(pl.multiple_of((item * PER + j) * HD, HD), HD)]
            s = SCALE * lax.dot_general(
                keys, q, (((1,), (1,)), ((), ())), preferred_element_type=jnp.float32
            )
            if own:
                key = lax.broadcasted_iota(jnp.int32, (BLK, BLK), 0)
                pos = lax.broadcasted_iota(jnp.int32, (BLK, BLK), 1)
                s = jnp.concatenate([jnp.where(key <= pos, s[:BLK], LOW), s[BLK:]], axis=0)
            scores[slot][:, j * BLK : (j + 1) * BLK] = s
            peaks[j] = s.reshape(KEYS // 8, 8, BLK).max(axis=0)

        def finish():
            for j in range(PER):
                peak = peaks[j].max(axis=0, keepdims=True)
                mx[slot, :, j * BLK : (j + 1) * BLK] = jnp.broadcast_to(peak, (8, BLK))

        return [functools.partial(part, j) for j in range(PER)], finish

    def weigh(item, slot, own=False):
        peak = mx[slot]
        if not own:
            before = m_ref[item]
            peak = jnp.maximum(before, peak)
            al[slot] = jnp.exp2(before - peak)
        m_ref[item] = peak

        def part(o):
            d = scores[slot][o : o + PIECE] - peak[0:1]
            probs[slot][o : o + PIECE] = jnp.exp2(d).astype(jnp.bfloat16)

        return [functools.partial(part, o) for o in range(0, KEYS, PIECE)]

    def mix(chunk, item, slot, own=False):
        def part(j):
            here = slice(j * BLK, (j + 1) * BLK)
            pv = jnp.dot(vt[chunk], probs[slot][:, here], preferred_element_type=jnp.float32)
            pv = pv[:AROWS]
            if not own:
                pv = acc_ref[item, :, here] * al[slot, 0:1, here] + pv
            acc_ref[item, :, here] = pv

        return [functools.partial(part, j) for j in range(PER)]

    def together(a, b, c):
        parts = []
        for order, group in enumerate((a, b, c)):
            for n, part in enumerate(group):
                parts.append(((n + 0.5) / len(group), order, part))
        for _, _, part in sorted(parts, key=lambda x: x[:2]):
            part()

    share = BLK // heads

    def out_columns(item):
        return pl.ds(pl.multiple_of((head * GROUP + item * PER) * HD, HD), PER * HD)

    def out_copy(item, step):
        peer = lax.rem(head + step, heads)
        return pltpu.make_async_remote_copy(
            src_ref=obuf.at[item, pl.ds(pl.multiple_of(peer * share, share), share)],
            dst_ref=out_ref.at[:, out_columns(item)],
            send_sem=out_send.at[item, step - 1],
            recv_sem=out_recv.at[item, step - 1],
            device_id=(me, peer),
            device_id_type=MESH,
        )

    def own_copy(item):
        return pltpu.make_async_copy(
            obuf.at[item, pl.ds(pl.multiple_of(head * share, share), share)],
            out_ref.at[:, out_columns(item)],
            own_sem.at[item],
        )

    def emit(item):
        for j in range(PER):
            a = acc_ref[item, :, j * BLK : (j + 1) * BLK]
            o = (a[:HD] / a[HD : HD + 1]).T.astype(jnp.bfloat16)
            obuf[item, :, j * HD : (j + 1) * HD] = o
        for step in (2, 1, 3):
            out_copy(item, step).start()
        own_copy(item).start()

    loads[3].wait()
    loop(0, col, lambda c: pltpu.make_async_copy(compact, kv.at[0, 4 + c], mate_recv.at[c]).wait())
    load_values(0, 4 + col)
    for t in range(ITEMS):
        a, finish = score(0, t, t % 2, own=True)
        b = weigh(t - 1, (t - 1) % 2, own=True) if t > 0 else []
        c = mix(0, t - 2, t % 2, own=True) if t > 1 else []
        together(a, b, c)
        finish()

    def pair(t, first=False):
        for n in range(2):
            p, item = walk(t + n + 2)
            pl.when(item == 0)(functools.partial(load_chunk, p))

            def step(n=n):
                a, finish = score(*where(t + n + 2), n)
                b = weigh(where(t + n + 1)[1], 1 - n, own=first and n == 0)
                c = mix(*where(t + n), n, own=first)
                together(a, b, c)
                finish()

            pl.when(t < total)(step)

    relay_singles()
    relay_bundle(3)
    relay_bundle(2)

    @pl.when(deep == 0)
    def _():
        relay_bundle(1)
        relay_bundle(0)

    pair(jnp.int32(ITEMS - 2), True)

    def body(n):
        t = 2 * n
        pl.when(jnp.logical_and(deep == 1, t == 4))(lambda: relay_bundle(1))
        pl.when(jnp.logical_and(deep == 1, t == 6))(lambda: relay_bundle(0))
        pair(t)
        done = t + 2 - major

        @pl.when(jnp.logical_and(done > 0, lax.rem(done, TAIL) == 0))
        def _():
            emit(lax.div(done, TAIL) - 1)

    loop(ITEMS // 2, lax.div(total, 2) - 1, body)
    together([], weigh(ITEMS - 1, 1), mix(*where(total - 2), 0))
    together([], [], mix(*where(total - 1), 1))
    emit(ITEMS - 1)

    def sent(copy):
        copy.wait_send()

    loop(col + 1, WIDTH, lambda c: sent(mate_copy(c)))

    pl.when(me == 0)(lambda: quarters(sent))

    loop(row + 1, rows, lambda r: sent(block_copy(r)))
    first_copies(sent)

    @pl.when(row > 0)
    def _():
        loop(BUNDLE * bundles, count, lambda s: to_near(functools.partial(single_copy, s), sent))
        early = jnp.minimum(bundles, 1)
        loop(0, early, lambda g: to_mates(functools.partial(bundle_copy, g), sent))
        loop(early, bundles, lambda g: to_near(functools.partial(bundle_copy, g), sent))

    @pl.when(twins)
    def _():
        twin_copy().wait_send()
        loop(jnp.maximum(row + 1, HALF), rows, lambda r: twin_along(r).wait_send())

    for item in range(ITEMS):
        own_copy(item).wait()
        for step in range(1, heads):
            out_copy(item, step).wait()


def per_device(shards, heads, query_rows, key_rows, value_rows, kept_rows):
    rows, depth = BLK // heads, shards // WIDTH
    f32, bf16, dma = jnp.float32, jnp.bfloat16, pltpu.SemaphoreType.DMA
    return pl.pallas_call(
        functools.partial(kernel, shards, heads),
        out_shape=jax.ShapeDtypeStruct((rows, heads * GROUP * HD), bf16),
        in_specs=[pl.BlockSpec(memory_space=pl.ANY)] * 4,
        out_specs=pl.BlockSpec(memory_space=pl.ANY),
        scratch_shapes=[
            pltpu.VMEM((BLK, GROUP * HD), bf16),
            pltpu.VMEM((BLK, HD), bf16),
            pltpu.VMEM((BLK, HD), bf16),
            pltpu.VMEM((1, KEEP), jnp.int32),
            pltpu.VMEM((KEEP, 2 * HD), bf16),
            pltpu.VMEM((KEEP, 2 * HD), bf16),
            pltpu.VMEM((CHUNKS, HALF, KEEP, 2 * HD), bf16),
            pltpu.VMEM((CHUNKS, VROWS, KEYS), bf16),
            pltpu.VMEM((KEYS, COLS), f32),
            pltpu.VMEM((KEYS, COLS), f32),
            pltpu.VMEM((KEYS, COLS), bf16),
            pltpu.VMEM((KEYS, COLS), bf16),
            pltpu.VMEM((2, 8, COLS), f32),
            pltpu.VMEM((2, 8, COLS), f32),
            pltpu.VMEM((ITEMS, 8, COLS), f32),
            pltpu.VMEM((ITEMS, AROWS, COLS), f32),
            pltpu.VMEM((ITEMS, BLK, PER * HD), bf16),
            dma((4,)),
            dma((depth,)),
            dma((WIDTH,)),
            dma((2, WIDTH)),
            dma((depth,)),
            dma((SLOTS, WIDTH - 1)),
            dma((SLOTS // BUNDLE, WIDTH - 1)),
            dma,
            dma((depth,)),
            dma,
            dma((WIDTH,)),
            dma((WIDTH, SLOTS)),
            dma((WIDTH, SLOTS // BUNDLE)),
            dma((ITEMS, heads - 1)),
            dma((ITEMS, heads - 1)),
            dma((ITEMS,)),
        ],
        compiler_params=pltpu.CompilerParams(
            collective_id=0, has_side_effects=True, vmem_limit_bytes=48 * 2**20
        ),
    )(query_rows, key_rows, value_rows, kept_rows.reshape(1, KEEP))


def solution(mesh):
    shards, heads = mesh.shape["ctx"], mesh.shape["head"]
    return jax.shard_map(
        functools.partial(per_device, shards, heads),
        mesh=mesh,
        in_specs=(P("ctx", "head"), P("ctx", "head"), P("ctx", "head"), P("ctx", "head", None)),
        out_specs=P(("ctx", "head"), None),
        check_vma=False,
    )
```

```python
import functools
import math

import jax
import jax.numpy as jnp
from jax import lax
from jax.experimental import pallas as pl
from jax.experimental.pallas import tpu as pltpu
from jax.sharding import PartitionSpec as P

MESH = pl.DeviceIdType.MESH
HD = 128
BLK = 256
KEEP = 64
GROUP = 16
PER = 4
ITEMS = GROUP // PER
COLS = PER * BLK
WIDTH = 4
SLOTS = 16
HALF = 8
KEYS = HALF * KEEP
CHUNKS = 1 + 2 * WIDTH
TAIL = 4
BUNDLE = 4
VROWS = 144
AROWS = 136
PIECE = 64
SCALE = math.log2(math.e) / math.sqrt(HD)
LOW = -1e30


def kernel(
    shards, heads, q_hbm, k_hbm, v_hbm, kept_hbm, out_ref,
    q_ref, k_ref, v_ref, kept_ref,
    compact, twin, kv, vt, s0, s1, p0, p1, mx, al, m_ref, acc_ref, obuf,
    load_sem, send_sem, mate_send, quarter_send, column_send, single_send, bundle_send, twin_send, along_send,
    twin_recv, mate_recv, slot_recv, bundle_recv, out_send, out_recv, own_sem,
):
    me = lax.axis_index("ctx")
    head = lax.axis_index("head")
    rows = shards // WIDTH
    row, col = lax.div(me, WIDTH), lax.rem(me, WIDTH)
    count = jnp.where(me > 0, row + 1, 0)
    bundles = lax.div(count, BUNDLE)
    deep = (count > HALF).astype(jnp.int32)
    scores, probs = (s0, s1), (p0, p1)

    barrier = pltpu.get_barrier_semaphore()

    def greet(block, to_head):
        pl.semaphore_signal(barrier, inc=1, device_id=(block, to_head), device_id_type=MESH)

    def mate(step):
        return row * WIDTH + lax.rem(col + step, WIDTH)

    def loop(low, high, body):
        def run(n, carry):
            body(n)
            return carry

        lax.fori_loop(low, high, run, 0)

    loop(0, row, lambda r: greet(r * WIDTH + col, head))
    for step in range(1, WIDTH):
        greet(mate(step), head)
    for step in range(1, heads):
        greet(me, lax.rem(head + step, heads))
    middle = rows // 2
    pl.when(jnp.logical_and(row == middle, col > 0))(lambda: greet(0, head))

    loads = [
        pltpu.make_async_copy(src, dst, load_sem.at[n])
        for n, (src, dst) in enumerate(
            ((kept_hbm, kept_ref), (k_hbm, k_ref), (v_hbm, v_ref), (q_hbm, q_ref))
        )
    ]
    for load in loads:
        load.start()
    for load in loads[:3]:
        load.wait()

    chosen = (
        lax.broadcasted_iota(jnp.int32, (BLK, KEEP), 0) == kept_ref[...]
    ).astype(jnp.bfloat16)
    for part, ref in ((0, k_ref), (HD, v_ref)):
        picked = lax.dot_general(
            chosen, ref[...], (((0,), (0,)), ((), ())), preferred_element_type=jnp.float32
        )
        compact[:, part : part + HD] = picked.astype(jnp.bfloat16)
    for n in range(BLK // KEEP):
        kv[0, n, :, :HD] = k_ref[n * KEEP : (n + 1) * KEEP, :]
        kv[0, n, :, HD:] = v_ref[n * KEEP : (n + 1) * KEEP, :]

    extra = jnp.where(me == 0, WIDTH - 1, 0)
    pl.semaphore_wait(barrier, rows - 1 - row + WIDTH - 1 + heads - 1 + extra)

    def remote(src, dst, send, recv, block):
        return pltpu.make_async_remote_copy(
            src_ref=src, dst_ref=dst, send_sem=send, recv_sem=recv,
            device_id=(block, head), device_id_type=MESH,
        )

    def slot_ref(c, s):
        return kv.at[1 + 2 * c + lax.div(s, HALF), lax.rem(s, HALF)]

    def bundle_ref(c, g):
        per = HALF // BUNDLE
        return kv.at[1 + 2 * c + lax.div(g, per), pl.ds(BUNDLE * lax.rem(g, per), BUNDLE)]

    def block_copy(r):
        return remote(
            compact, slot_ref(col, row + 1), send_sem.at[r], slot_recv.at[col, row + 1],
            r * WIDTH + col,
        )

    def mate_copy(c):
        return remote(
            compact, kv.at[0, 4 + col], mate_send.at[c], mate_recv.at[col], row * WIDTH + c
        )

    def quarter_copy(c, r):
        return remote(
            kv.at[0, c], slot_ref(c, 0), quarter_send.at[lax.div(r, middle), c],
            slot_recv.at[c, 0], r * WIDTH + c,
        )

    def quarters(do):
        for c in range(WIDTH):
            do(quarter_copy(c, middle))
        for c in range(1, WIDTH):
            do(quarter_copy(c, 0))

    def column_copy(source, r):
        return remote(
            source, slot_ref(col, 0), column_send.at[r], slot_recv.at[col, 0], r * WIDTH + col
        )

    loop(col + 1, WIDTH, lambda c: mate_copy(c).start())

    pl.when(me == 0)(lambda: quarters(lambda copy: copy.start()))

    opposite = lax.rem(col + 2, WIDTH)
    twins = jnp.logical_and(row >= HALF - 1, row < rows - 1)

    def twin_copy():
        return remote(compact, twin, twin_send, twin_recv, mate(2))

    def twin_along(r):
        return remote(
            twin, slot_ref(opposite, row + 1), along_send.at[r], slot_recv.at[opposite, row + 1],
            r * WIDTH + col,
        )

    def target(n):
        plain = rows - 1 - n
        turned = jnp.where(n == 2, rows - 1, jnp.where(n < 2, plain - 1, plain))
        return jnp.where(row < rows - 3, turned, plain)

    pl.when(twins)(lambda: twin_copy().start())
    loop(0, rows - 1 - row, lambda n: block_copy(target(n)).start())

    filler = jnp.concatenate(
        [jnp.broadcast_to(k_ref[0:1, :], (KEEP, HD)), jnp.zeros((KEEP, HD), jnp.bfloat16)], axis=1
    )

    def fill_mate(c):
        kv[0, 4 + c] = filler

    def fill_slot(s):
        for c in range(WIDTH):
            kv[1 + 2 * c + lax.div(s, HALF), lax.rem(s, HALF)] = filler

    loop(col, WIDTH, fill_mate)
    loop(count, SLOTS, fill_slot)

    def wait_slot(c, s):
        pltpu.make_async_copy(compact, slot_ref(c, s), slot_recv.at[c, s]).wait()

    def single_copy(s, step):
        return remote(
            slot_ref(col, s), slot_ref(col, s), single_send.at[s, step - 1], slot_recv.at[col, s],
            mate(step),
        )

    def bundle_copy(g, step):
        return remote(
            bundle_ref(col, g), bundle_ref(col, g), bundle_send.at[g, step - 1],
            bundle_recv.at[col, g], mate(step),
        )

    def to_mates(copy, do):
        for step in (1, 3, 2):
            do(copy(step))

    def to_near(copy, do):
        for step in (1, 3):
            do(copy(step))
        pl.when(deep == 0)(lambda: do(copy(2)))

    def start(copy):
        copy.start()

    def zero_copy(step):
        return remote(
            kv.at[0, 0], slot_ref(0, 0), single_send.at[0, step - 1], slot_recv.at[0, 0], mate(step)
        )

    gives = jnp.logical_or(row == 0, row == middle)

    def first_copies(do):
        def along(source):
            loop(1, middle, lambda n: do(column_copy(source, row + middle - n)))

        pl.when(me == 0)(lambda: along(kv.at[0, 0]))
        pl.when(jnp.logical_and(gives, me > 0))(lambda: along(slot_ref(col, 0)))

        pl.when(me == 0)(lambda: to_mates(zero_copy, do))

        @pl.when(jnp.logical_and(row == 0, me > 0))
        def _():
            for step in (1, 3, 2):
                pl.when(mate(step) > 0)(lambda: do(single_copy(0, step)))

    pl.when(jnp.logical_and(gives, me > 0))(lambda: wait_slot(col, 0))
    first_copies(start)

    @pl.when(twins)
    def _():
        twin_copy().wait_recv()
        loop(0, rows - 1 - row, lambda n: twin_along(rows - 1 - n).start())

    def relay_singles():
        def one(n):
            slot = count - 1 - n
            wait_slot(col, slot)
            to_near(functools.partial(single_copy, slot), start)

        pl.when(row > 0)(lambda: loop(0, count - BUNDLE * bundles, one))

    def relay_bundle(g):
        @pl.when(g < bundles)
        def _():
            pl.when(jnp.logical_or(g > 0, row != middle))(lambda: wait_slot(col, BUNDLE * g))
            for b in range(1, BUNDLE):
                wait_slot(col, BUNDLE * g + b)
            (to_mates if g < HALF // BUNDLE else to_near)(functools.partial(bundle_copy, g), start)

    def wait_relayed(c, half):
        def many(g):
            pltpu.make_async_copy(bundle_ref(c, g), bundle_ref(c, g), bundle_recv.at[c, g]).wait()

        whole = jnp.where(jnp.logical_and(c == opposite, half == 1), HALF // BUNDLE, bundles)
        low = jnp.maximum(BUNDLE * whole, HALF * half)
        loop(low, jnp.minimum(count, HALF * half + HALF), lambda s: wait_slot(c, s))
        loop(2 * half, jnp.minimum(whole, 2 * half + 2), many)

    def place(p):
        own = 1 + deep
        k = lax.rem(jnp.maximum(p - 1 - own, 0), WIDTH - 1)
        step = jnp.where(p > own, 1 + 2 * (k == 1).astype(jnp.int32) + (k == 2).astype(jnp.int32), 0)
        late = jnp.logical_or(p == 1, jnp.logical_and(p > own, p < own + WIDTH))
        return lax.rem(col + step, WIDTH), deep * late.astype(jnp.int32)

    def chunk_of(p):
        c, half = place(p)
        return jnp.where(p > 0, 1 + 2 * c + half, 0)

    def load_values(chunk, limit):
        vt[chunk, 0:HD] = kv[chunk].reshape(KEYS, 2 * HD)[:, HD:].T
        valid = lax.broadcasted_iota(jnp.int32, (VROWS - HD, KEYS), 1) < limit * KEEP
        vt[chunk, HD:VROWS] = valid.astype(jnp.bfloat16)

    def load_chunk(p):
        c, half = place(p)
        pl.when(c != col)(lambda: wait_relayed(c, half))
        load_values(1 + 2 * c + half, count - HALF * half)

    chunks = 1 + WIDTH * (1 + deep)
    major = ITEMS * (chunks - TAIL)
    total = ITEMS * chunks

    def walk(t):
        late = t - major
        p = jnp.where(late < 0, lax.div(t, ITEMS), chunks - TAIL + lax.rem(late, TAIL))
        item = jnp.where(late < 0, lax.rem(t, ITEMS), lax.div(late, TAIL))
        return p, item

    def where(t):
        p, item = walk(t)
        return chunk_of(p), item

    def score(chunk, item, slot, own=False):
        keys = kv[chunk].reshape(KEYS, 2 * HD)[:, :HD]
        peaks = {}

        def part(j):
            q = q_ref[:, pl.ds(pl.multiple_of((item * PER + j) * HD, HD), HD)]
            s = SCALE * lax.dot_general(
                keys, q, (((1,), (1,)), ((), ())), preferred_element_type=jnp.float32
            )
            if own:
                key = lax.broadcasted_iota(jnp.int32, (BLK, BLK), 0)
                pos = lax.broadcasted_iota(jnp.int32, (BLK, BLK), 1)
                s = jnp.concatenate([jnp.where(key <= pos, s[:BLK], LOW), s[BLK:]], axis=0)
            scores[slot][:, j * BLK : (j + 1) * BLK] = s
            peaks[j] = s.reshape(KEYS // 8, 8, BLK).max(axis=0)

        def finish():
            for j in range(PER):
                peak = peaks[j].max(axis=0, keepdims=True)
                mx[slot, :, j * BLK : (j + 1) * BLK] = jnp.broadcast_to(peak, (8, BLK))

        return [functools.partial(part, j) for j in range(PER)], finish

    def weigh(item, slot, own=False):
        peak = mx[slot]
        if not own:
            before = m_ref[item]
            peak = jnp.maximum(before, peak)
            al[slot] = jnp.exp2(before - peak)
        m_ref[item] = peak

        def part(o):
            d = scores[slot][o : o + PIECE] - peak[0:1]
            probs[slot][o : o + PIECE] = jnp.exp2(d).astype(jnp.bfloat16)

        return [functools.partial(part, o) for o in range(0, KEYS, PIECE)]

    def mix(chunk, item, slot, own=False):
        def part(j):
            here = slice(j * BLK, (j + 1) * BLK)
            pv = jnp.dot(vt[chunk], probs[slot][:, here], preferred_element_type=jnp.float32)
            pv = pv[:AROWS]
            if not own:
                pv = acc_ref[item, :, here] * al[slot, 0:1, here] + pv
            acc_ref[item, :, here] = pv

        return [functools.partial(part, j) for j in range(PER)]

    def together(a, b, c):
        parts = []
        for order, group in enumerate((a, b, c)):
            for n, part in enumerate(group):
                parts.append(((n + 0.5) / len(group), order, part))
        for _, _, part in sorted(parts, key=lambda x: x[:2]):
            part()

    share = BLK // heads

    def out_columns(item):
        return pl.ds(pl.multiple_of((head * GROUP + item * PER) * HD, HD), PER * HD)

    def out_copy(item, step):
        peer = lax.rem(head + step, heads)
        return pltpu.make_async_remote_copy(
            src_ref=obuf.at[item, pl.ds(pl.multiple_of(peer * share, share), share)],
            dst_ref=out_ref.at[:, out_columns(item)],
            send_sem=out_send.at[item, step - 1],
            recv_sem=out_recv.at[item, step - 1],
            device_id=(me, peer),
            device_id_type=MESH,
        )

    def own_copy(item):
        return pltpu.make_async_copy(
            obuf.at[item, pl.ds(pl.multiple_of(head * share, share), share)],
            out_ref.at[:, out_columns(item)],
            own_sem.at[item],
        )

    def emit(item):
        for j in range(PER):
            a = acc_ref[item, :, j * BLK : (j + 1) * BLK]
            o = (a[:HD] / a[HD : HD + 1]).T.astype(jnp.bfloat16)
            obuf[item, :, j * HD : (j + 1) * HD] = o
        for step in (2, 1, 3):
            out_copy(item, step).start()
        own_copy(item).start()

    loads[3].wait()
    loop(0, col, lambda c: pltpu.make_async_copy(compact, kv.at[0, 4 + c], mate_recv.at[c]).wait())
    load_values(0, 4 + col)
    for t in range(ITEMS):
        a, finish = score(0, t, t % 2, own=True)
        b = weigh(t - 1, (t - 1) % 2, own=True) if t > 0 else []
        c = mix(0, t - 2, t % 2, own=True) if t > 1 else []
        together(a, b, c)
        finish()

    def pair(t, first=False):
        for n in range(2):
            p, item = walk(t + n + 2)
            pl.when(item == 0)(functools.partial(load_chunk, p))

            def step(n=n):
                a, finish = score(*where(t + n + 2), n)
                b = weigh(where(t + n + 1)[1], 1 - n, own=first and n == 0)
                c = mix(*where(t + n), n, own=first)
                together(a, b, c)
                finish()

            pl.when(t < total)(step)

    relay_singles()
    relay_bundle(3)
    relay_bundle(2)

    @pl.when(deep == 0)
    def _():
        relay_bundle(1)
        relay_bundle(0)

    pair(jnp.int32(ITEMS - 2), True)

    def body(n):
        t = 2 * n
        pl.when(jnp.logical_and(deep == 1, t == 4))(lambda: relay_bundle(1))
        pl.when(jnp.logical_and(deep == 1, t == 6))(lambda: relay_bundle(0))
        pair(t)
        done = t + 2 - major

        @pl.when(jnp.logical_and(done > 0, lax.rem(done, TAIL) == 0))
        def _():
            emit(lax.div(done, TAIL) - 1)

    loop(ITEMS // 2, lax.div(total, 2) - 1, body)
    together([], weigh(ITEMS - 1, 1), mix(*where(total - 2), 0))
    together([], [], mix(*where(total - 1), 1))
    emit(ITEMS - 1)

    def sent(copy):
        copy.wait_send()

    loop(col + 1, WIDTH, lambda c: sent(mate_copy(c)))

    pl.when(me == 0)(lambda: quarters(sent))

    loop(row + 1, rows, lambda r: sent(block_copy(r)))
    first_copies(sent)

    @pl.when(row > 0)
    def _():
        loop(BUNDLE * bundles, count, lambda s: to_near(functools.partial(single_copy, s), sent))
        early = jnp.minimum(bundles, HALF // BUNDLE)
        loop(0, early, lambda g: to_mates(functools.partial(bundle_copy, g), sent))
        loop(early, bundles, lambda g: to_near(functools.partial(bundle_copy, g), sent))

    @pl.when(twins)
    def _():
        twin_copy().wait_send()
        loop(row + 1, rows, lambda r: twin_along(r).wait_send())

    for item in range(ITEMS):
        own_copy(item).wait()
        for step in range(1, heads):
            out_copy(item, step).wait()


def per_device(shards, heads, query_rows, key_rows, value_rows, kept_rows):
    rows, depth = BLK // heads, shards // WIDTH
    f32, bf16, dma = jnp.float32, jnp.bfloat16, pltpu.SemaphoreType.DMA
    return pl.pallas_call(
        functools.partial(kernel, shards, heads),
        out_shape=jax.ShapeDtypeStruct((rows, heads * GROUP * HD), bf16),
        in_specs=[pl.BlockSpec(memory_space=pl.ANY)] * 4,
        out_specs=pl.BlockSpec(memory_space=pl.ANY),
        scratch_shapes=[
            pltpu.VMEM((BLK, GROUP * HD), bf16),
            pltpu.VMEM((BLK, HD), bf16),
            pltpu.VMEM((BLK, HD), bf16),
            pltpu.VMEM((1, KEEP), jnp.int32),
            pltpu.VMEM((KEEP, 2 * HD), bf16),
            pltpu.VMEM((KEEP, 2 * HD), bf16),
            pltpu.VMEM((CHUNKS, HALF, KEEP, 2 * HD), bf16),
            pltpu.VMEM((CHUNKS, VROWS, KEYS), bf16),
            pltpu.VMEM((KEYS, COLS), f32),
            pltpu.VMEM((KEYS, COLS), f32),
            pltpu.VMEM((KEYS, COLS), bf16),
            pltpu.VMEM((KEYS, COLS), bf16),
            pltpu.VMEM((2, 8, COLS), f32),
            pltpu.VMEM((2, 8, COLS), f32),
            pltpu.VMEM((ITEMS, 8, COLS), f32),
            pltpu.VMEM((ITEMS, AROWS, COLS), f32),
            pltpu.VMEM((ITEMS, BLK, PER * HD), bf16),
            dma((4,)),
            dma((depth,)),
            dma((WIDTH,)),
            dma((2, WIDTH)),
            dma((depth,)),
            dma((SLOTS, WIDTH - 1)),
            dma((SLOTS // BUNDLE, WIDTH - 1)),
            dma,
            dma((depth,)),
            dma,
            dma((WIDTH,)),
            dma((WIDTH, SLOTS)),
            dma((WIDTH, SLOTS // BUNDLE)),
            dma((ITEMS, heads - 1)),
            dma((ITEMS, heads - 1)),
            dma((ITEMS,)),
        ],
        compiler_params=pltpu.CompilerParams(
            collective_id=0, has_side_effects=True, vmem_limit_bytes=48 * 2**20
        ),
    )(query_rows, key_rows, value_rows, kept_rows.reshape(1, KEEP))


def solution(mesh):
    shards, heads = mesh.shape["ctx"], mesh.shape["head"]
    return jax.shard_map(
        functools.partial(per_device, shards, heads),
        mesh=mesh,
        in_specs=(P("ctx", "head"), P("ctx", "head"), P("ctx", "head"), P("ctx", "head", None)),
        out_specs=P(("ctx", "head"), None),
        check_vma=False,
    )
```
